512 devices in a mesh: group: 16 (over x, z_lo, core), loop: 32 (over y, z_hi).
Axes of the slice: x: 4, y: 8, z: 8 (z_hi: 4, z_lo: 2; z = z_hi * 2 + z_lo), core: 2. Of those that a mesh axis runs over, the one named last changes fastest.
Arguments:
- tile_vals: bfloat16 [16, 32, 32, 128, 128], P('group', 'loop'), may hold values from 0 to 1
- tile_rows: int32 [16, 32, 32], P('group', 'loop'), may hold values from 0 to 15, as said below
- tile_cols: int32 [16, 32, 32], P('group', 'loop'), may hold values from 0 to 15, as said below
- tile_count: int32 [16, 32], P('group', 'loop'), may hold values from 8 to 32, as said below
- start_panel: float32 [32, 2048, 64], P('loop', 'group'), may hold values from -6 to 6
Outputs:
- session_panel: float32 [32, 2048, 64], P('loop', 'group')
- attendee_panel: float32 [16, 2048, 64], P('group', 'loop')
The draws below stay inside these ranges and needn't reach their ends.
Inputs may be any that keep to these rules, and one draw needn't show every extreme that they name: `tile_count`: 32 is reached in every draw, at a block drawn from the seed. Within one block, the 32 slots name distinct pairs of tile_rows and tile_cols. Within one block, the 32 slots name distinct pairs of tile_rows and tile_cols.
All inputs are finite; a program needn't handle non-finite values.
Results may differ from the reference program's by a relative error of at most 0.0054.
Values may be sent and summed in bfloat16 or wider, within the bound.
No kernel may reach another device: no remote copies, remote signals or barrier semaphores. Data moves between devices by JAX's collectives and lax.ppermute only.
A program may use at most 64 MiB of HBM per device.

```python
import jax
import jax.numpy as jnp
from jax import lax

TILE = 128
PANEL = 64
ROWS_DEV = 2048
COLS_DEV = 2048
NT = 32
ITERS = 3
N_GROUP = 16
N_LOOP = 32


def tile_cells(key):
    cell_total = ROWS_DEV // TILE * (COLS_DEV // TILE)
    block_keys = jax.random.split(key, N_GROUP * N_LOOP)
    chosen = jax.vmap(lambda block_key: jax.random.permutation(block_key, cell_total)[:NT])(block_keys)
    return chosen.reshape(N_GROUP, N_LOOP, NT).astype(jnp.int32)


def draw_tile_rows(key, part):
    chosen = tile_cells(key)
    return (chosen // (COLS_DEV // TILE)).astype(jnp.int32)


def draw_tile_cols(key, part):
    chosen = tile_cells(key)
    return (chosen % (COLS_DEV // TILE)).astype(jnp.int32)


def draw_tile_count(key, part):
    key = jax.random.fold_in(key, 7)
    first_key, second_key = jax.random.split(key)
    counts = jax.random.randint(first_key, (N_GROUP * N_LOOP,), NT // 4, NT + 1)
    chosen_spot = jax.random.randint(second_key, (), 0, N_GROUP * N_LOOP)
    counts = jnp.where(jnp.arange(N_GROUP * N_LOOP) == chosen_spot, NT, counts)
    return counts.reshape(N_GROUP, N_LOOP).astype(jnp.int32)


def levels(own_key, dims, pieces, least, high):
    gain = 1.0
    for axis_at, shards_of in pieces:
        steps = jax.random.uniform(jax.random.fold_in(jax.random.fold_in(own_key, 6), axis_at), (shards_of,), jnp.float32, least / len(pieces), high / len(pieces))
        gain = gain * jnp.repeat(jnp.exp(steps), dims[axis_at] // shards_of).reshape((-1,) + (1,) * (len(dims) - 1 - axis_at))
    return gain


def scatter_about(key, dims, scale, most, shards=(), held_as=jnp.bfloat16):
    factor_of = levels(key, dims, shards, -0.22, 0.18) if shards else 1.0
    entries = jax.random.normal(key, dims, jnp.float32) * scale * factor_of
    return jnp.minimum(jnp.maximum(entries, -most), most).astype(held_as)


def setup_inputs(seed: int = 0) -> dict:
    key_list = jax.random.split(jax.random.key(seed), 6)
    tile_vals = jnp.clip(1.0 * jax.random.uniform(key_list[0], (N_GROUP, N_LOOP, NT, TILE, TILE), jnp.float32) ** levels(key_list[0], (N_GROUP, N_LOOP, NT, TILE, TILE), ((0, 16), (1, 32)), -0.2, 0.2), 0.0, 1.0).astype(jnp.bfloat16)
    tile_rows = draw_tile_rows(jax.random.fold_in(key_list[5], 71), 0)
    tile_cols = draw_tile_cols(jax.random.fold_in(key_list[5], 71), 0)
    tile_count = draw_tile_count(jax.random.fold_in(key_list[5], 71), 0)
    start_panel = scatter_about(key_list[4], (N_LOOP, COLS_DEV, PANEL), 1.0, 6.0, ((0, 32), (1, 16)), jnp.float32)
    return {"tile_vals": tile_vals, "tile_rows": tile_rows, "tile_cols": tile_cols, "tile_count": tile_count, "start_panel": start_panel}


def orthonormal(stacked, gram_sum):
    factor = jnp.linalg.cholesky(gram_sum)
    return jax.scipy.linalg.solve_triangular(factor, stacked.T, lower=True).T

def reference(tile_vals, tile_rows, tile_cols, tile_count, start_panel):
    highest = lax.Precision.HIGHEST
    row_blocks = ROWS_DEV // TILE
    col_blocks = COLS_DEV // TILE
    alive_mask = (jnp.arange(NT)[None, None, :] < tile_count[:, :, None]).astype(jnp.float32)

    def row_degree_group(group_id):

        def one_block(loop_id):
            tiles = tile_vals[group_id, loop_id].astype(jnp.float32) * alive_mask[group_id, loop_id][:, None, None]
            onehot = (tile_rows[group_id, loop_id][None, :] == jnp.arange(row_blocks)[:, None]).astype(jnp.float32)
            return jnp.dot(onehot, lax.optimization_barrier(jnp.sum(tiles, axis=2)), precision=highest)
        return lax.optimization_barrier(jnp.sum(lax.map(one_block, jnp.arange(N_LOOP)), axis=0)).reshape(ROWS_DEV)

    def col_degree_loop(loop_id):

        def one_block(group_id):
            tiles = tile_vals[group_id, loop_id].astype(jnp.float32) * alive_mask[group_id, loop_id][:, None, None]
            onehot = (tile_cols[group_id, loop_id][None, :] == jnp.arange(col_blocks)[:, None]).astype(jnp.float32)
            return jnp.dot(onehot, lax.optimization_barrier(jnp.sum(tiles, axis=1)), precision=highest)
        return lax.optimization_barrier(jnp.sum(lax.map(one_block, jnp.arange(N_GROUP)), axis=0)).reshape(COLS_DEV)
    row_scale = lax.rsqrt(lax.map(row_degree_group, jnp.arange(N_GROUP)) + 1.0)
    col_scale = lax.rsqrt(lax.map(col_degree_loop, jnp.arange(N_LOOP)) + 1.0)
    panel = start_panel
    attendee = jnp.zeros((N_GROUP, ROWS_DEV, PANEL), jnp.float32)
    for iteration in range(ITERS):
        session_blocks = (panel * col_scale[:, :, None]).astype(jnp.bfloat16).reshape(N_LOOP, col_blocks, TILE, PANEL)

        def forward_group(group_id):

            def forward_block(loop_id):
                chosen = jnp.take(session_blocks[loop_id], tile_cols[group_id, loop_id], axis=0).astype(jnp.float32)
                product = jnp.einsum('tij,tjk->tik', tile_vals[group_id, loop_id].astype(jnp.float32), chosen)
                product = product * alive_mask[group_id, loop_id][:, None, None]
                onehot = (tile_rows[group_id, loop_id][None, :] == jnp.arange(row_blocks)[:, None]).astype(jnp.float32)
                return jnp.einsum('rt,tik->rik', onehot, product, precision=highest)
            return lax.optimization_barrier(jnp.sum(lax.map(forward_block, jnp.arange(N_LOOP)), axis=0))
        summed = lax.map(forward_group, jnp.arange(N_GROUP)).reshape(N_GROUP, ROWS_DEV, PANEL)
        summed = summed * row_scale[:, :, None]
        stacked = summed.reshape(N_GROUP * ROWS_DEV, PANEL)
        gram_sum = jnp.dot(stacked.T, stacked, precision=highest)
        attendee = orthonormal(stacked, gram_sum).reshape(N_GROUP, ROWS_DEV, PANEL)
        attendee_blocks = (attendee * row_scale[:, :, None]).astype(jnp.bfloat16).reshape(N_GROUP, row_blocks, TILE, PANEL)

        def backward_loop(loop_id):

            def backward_block(group_id):
                chosen = jnp.take(attendee_blocks[group_id], tile_rows[group_id, loop_id], axis=0).astype(jnp.float32)
                product = jnp.einsum('tij,tik->tjk', tile_vals[group_id, loop_id].astype(jnp.float32), chosen)
                product = product * alive_mask[group_id, loop_id][:, None, None]
                onehot = (tile_cols[group_id, loop_id][None, :] == jnp.arange(col_blocks)[:, None]).astype(jnp.float32)
                return jnp.einsum('rt,tik->rik', onehot, product, precision=highest)
            return lax.optimization_barrier(jnp.sum(lax.map(backward_block, jnp.arange(N_GROUP)), axis=0))
        summed_cols = lax.map(backward_loop, jnp.arange(N_LOOP)).reshape(N_LOOP, COLS_DEV, PANEL)
        summed_cols = summed_cols * col_scale[:, :, None]
        stacked_cols = summed_cols.reshape(N_LOOP * COLS_DEV, PANEL)
        gram_cols = jnp.dot(stacked_cols.T, stacked_cols, precision=highest)
        panel = orthonormal(stacked_cols, gram_cols).reshape(N_LOOP, COLS_DEV, PANEL)
    return (panel, attendee)
```

```python
import functools

import jax
import jax.numpy as jnp
from jax import lax
from jax.experimental import pallas as pl
from jax.experimental.pallas import tpu as pltpu
from jax.sharding import PartitionSpec as P

ITERS = 3
SIDE = 128
WIDTH = 64
LANES = 128
GRAM_ROWS = 48
DEGREE_ROWS = 16
F32 = jnp.float32
BF16 = jnp.bfloat16
HIGHEST = lax.Precision.HIGHEST


def iota(shape, dim):
    return lax.broadcasted_iota(jnp.int32, shape, dim)


def halves_to_rows(packed):
    return jnp.concatenate([packed[:, :WIDTH], packed[:, WIDTH:]], axis=0)


def rows_to_halves(rows):
    half = rows.shape[0] // 2
    return jnp.concatenate([rows[:half], rows[half:]], axis=1)


def lanes_to_packed(row, half):
    shape = (half, LANES)
    spread = jnp.broadcast_to(row, shape)
    delta = iota(shape, 1) - iota(shape, 0)
    first = jnp.sum(jnp.where(delta == 0, spread, 0.0), axis=1, keepdims=True)
    last = jnp.sum(jnp.where(delta == half, spread, 0.0), axis=1, keepdims=True)
    return jnp.where(iota(shape, 1) < WIDTH, first, last)


def split_two(value):
    high = value.astype(BF16).astype(F32)
    return high, value - high


def diagonal_blocks(square):
    return square[:WIDTH, :WIDTH] + square[WIDTH:, WIDTH:]


def inverse_factor(gram):
    eye = (iota((WIDTH, WIDTH), 0) == iota((WIDTH, WIDTH), 1)).astype(F32)
    whole = jnp.concatenate([gram, eye], axis=1)
    blocks = [whole[8 * b : 8 * b + 8] for b in range(WIDTH // 8)]
    below = iota((8, 1), 0)
    for k in range(WIDTH):
        at, inner = k // 8, k % 8
        row = blocks[at][inner : inner + 1]
        row = row * (1.0 / row[:, k : k + 1])
        for b in range(at, WIDTH // 8):
            if b == at and inner == 7:
                continue
            column = blocks[b][:, k : k + 1]
            if b == at:
                column = jnp.where(below > inner, column, 0.0)
            blocks[b] = blocks[b] - column * row
    whole = jnp.concatenate(blocks, axis=0)
    pivots = jnp.sum(whole[:, :WIDTH] * eye, axis=1, keepdims=True)
    return whole[:, WIDTH:] * lax.rsqrt(pivots)


def apply_factor(packed, inverse):
    zero = jnp.zeros((WIDTH, WIDTH), F32)
    both = jnp.concatenate(
        [
            jnp.concatenate([inverse, zero], axis=1),
            jnp.concatenate([zero, inverse], axis=1),
        ],
        axis=0,
    )
    return lax.dot_general(
        packed, both, (((1,), (1,)), ((), ())), precision=HIGHEST, preferred_element_type=F32
    )


def gram_to_message(gram):
    shape = (WIDTH, WIDTH)
    high, low = split_two(gram)
    mixed = jnp.where(iota(shape, 0) >= iota(shape, 1), high, low.T)
    diagonal = jnp.sum(jnp.where(iota(shape, 0) == iota(shape, 1), low, 0.0), axis=0, keepdims=True)
    diagonal = jnp.concatenate([diagonal, diagonal], axis=1)
    return rows_to_halves(mixed), jnp.broadcast_to(diagonal, (16, LANES))


def message_to_gram(mixed, diagonal):
    shape = (WIDTH, WIDTH)
    square = halves_to_rows(mixed)
    on_diagonal = iota(shape, 0) == iota(shape, 1)
    return jnp.where(on_diagonal, square + diagonal[:1, :WIDTH], square + square.T)


def degree_kernel(row_at, col_at, values, col_degree, row_degree, col_sum, row_sum):
    col_sum[...] = jnp.zeros_like(col_sum)
    row_sum[...] = jnp.zeros_like(row_sum)
    ones = jnp.ones((8, SIDE), BF16)
    for t in range(values.shape[0]):
        tile = values[t]
        col_sum[col_at[t]] += jnp.dot(ones, tile, preferred_element_type=F32)
        row_sum[row_at[t]] += lax.dot_general(
            ones, tile, (((1,), (1,)), ((), ())), preferred_element_type=F32
        )
    for b in range(col_degree.shape[0]):
        col_degree[b : b + 1] = col_sum[b, :1]
        row_degree[b : b + 1] = row_sum[b, :1]


def product_kernel(kind, n_from, rows_from, n_to, rows_to, *refs):
    if kind == "start":
        source, target, gathered, tiles, extra, out, weight, spread, total = refs
    elif kind == "degree":
        source, target, gathered, tiles, out, weight, spread, total = refs
    else:
        source, target, gathered, tiles, weight, out, spread, total = refs
    lane_low = iota((SIDE // 2, LANES), 1) < WIDTH
    n_blocks = total.shape[0] - 1
    per_block = SIDE // 2 // rows_from

    if kind == "start":
        degree = 1.0 + jnp.sum(gathered[:, rows_from:, :], axis=0)

    grams = jnp.zeros((2 * LANES, LANES), F32)
    for b in range(n_blocks):
        rows = slice(b * SIDE // 2, (b + 1) * SIDE // 2)
        if kind == "start":
            packed_degree = lanes_to_packed(degree[b : b + 1], SIDE // 2)
            weight[rows] = packed_degree
            panel = (gathered[b, :rows_from] * lax.rsqrt(packed_degree)).astype(BF16).astype(F32)
        else:
            parts = [
                gathered[b * per_block + j, :rows_from].astype(F32) for j in range(per_block)
            ]
            panel = parts[0] if per_block == 1 else jnp.concatenate(parts, axis=0)
        if kind == "degree":
            packs = []
            for j in range(per_block):
                pieces = gathered[b * per_block + j, rows_from:].astype(F32)
                packs.append(lanes_to_packed(jnp.sum(pieces[:3], axis=0, keepdims=True), rows_from))
            packed_degree = packs[0] if per_block == 1 else jnp.concatenate(packs, axis=0)
            weight[rows] = packed_degree
        turned = pltpu.roll(panel, WIDTH, 1)
        half = SIDE // 2
        spread[b, :half] = jnp.where(lane_low, panel, 0.0).astype(BF16)
        spread[b, half : 2 * half] = jnp.where(lane_low, turned, 0.0).astype(BF16)
        spread[b, 2 * half : 3 * half] = jnp.where(lane_low, 0.0, turned).astype(BF16)
        spread[b, 3 * half :] = jnp.where(lane_low, 0.0, panel).astype(BF16)
        if kind != "start":
            high, low = split_two(panel * weight[rows])
            both = jnp.concatenate([high, low], axis=1).astype(BF16)
            grams = grams + lax.dot_general(
                both, panel.astype(BF16), (((0,), (0,)), ((), ())), preferred_element_type=F32
            )
        total[b] = jnp.zeros((half, LANES), F32)
    total[n_blocks] = jnp.zeros((half, LANES), F32)

    for t in range(tiles.shape[0]):
        total[target[t]] += jnp.dot(tiles[t], spread[source[t]], preferred_element_type=F32)

    if kind == "start":
        message = extra[...]
    else:
        gram = diagonal_blocks(grams[:LANES]) + diagonal_blocks(grams[LANES:])
        mixed, diagonal = gram_to_message(gram)
        mixed, diagonal = mixed.astype(BF16), diagonal.astype(BF16)
    to_block = SIDE // 2 // rows_to
    for d in range(n_to):
        first = d % to_block * rows_to
        out[d, :rows_to] = total[d // to_block, first : first + rows_to].astype(BF16)
        if kind == "start":
            out[d, rows_to:] = message[d]
        else:
            out[d, rows_to : rows_to + 32] = mixed
            out[d, rows_to + 32 :] = diagonal


def sum_kernel(kind, n_from, rows, n_copies, *refs):
    if kind == "degree":
        received, copies, summed_out, scale_out = refs
    elif kind == "plain":
        received, scale_ref, copies, summed_out = refs
    else:
        received, scale_ref, other, copies, summed_out, other_out = refs
    summed = received[0].astype(F32)
    for s in range(1, n_from):
        summed = summed + received[s].astype(F32)
    panel = summed[:rows]
    if kind == "degree":
        pieces = summed[rows:]
        degree = 1.0 + jnp.sum(pieces[:3], axis=0, keepdims=True)
        scale = lax.rsqrt(lanes_to_packed(degree, rows))
        scale_out[...] = scale
        panel = panel * scale
    else:
        scale = scale_ref[...]
        gram = message_to_gram(summed[rows : rows + 32], summed[rows + 32 :])
        inverse = inverse_factor(gram)
        panel = apply_factor(panel * scale, inverse)
    summed_out[...] = panel
    if kind == "last":
        other_out[...] = halves_to_rows(apply_factor(other[...], inverse))
        square = lax.dot_general(
            panel, panel, (((0,), (0,)), ((), ())), precision=HIGHEST, preferred_element_type=F32
        )
        message = rows_to_halves(diagonal_blocks(square))
    else:
        message = (panel * scale).astype(BF16)
    for d in range(n_copies):
        copies[d, : message.shape[0]] = message
    if kind == "degree":
        high, rest = split_two(degree)
        middle, low = split_two(rest)
        at = iota((DEGREE_ROWS, LANES), 0)
        tail = jnp.where(at == 0, high, jnp.where(at == 1, middle, jnp.where(at == 2, low, 0.0)))
        tail = tail.astype(BF16)
        for d in range(n_copies):
            copies[d, rows:] = tail


def last_kernel(n_from, received, panel, out):
    summed = received[0]
    for s in range(1, n_from):
        summed = summed + received[s]
    inverse = inverse_factor(halves_to_rows(summed))
    out[...] = halves_to_rows(apply_factor(panel[...], inverse))


VMEM = pl.BlockSpec(memory_space=pltpu.VMEM)
SMEM = pl.BlockSpec(memory_space=pltpu.SMEM)


def call(kernel, name, in_specs, out_shapes, scratch=()):
    return pl.pallas_call(
        kernel,
        name=name,
        in_specs=in_specs,
        out_specs=[VMEM] * len(out_shapes),
        out_shape=[jax.ShapeDtypeStruct(s, d) for s, d in out_shapes],
        scratch_shapes=list(scratch),
        compiler_params=pltpu.CompilerParams(vmem_limit_bytes=32 * 1024 * 1024),
    )


def exchange(array, axis):
    n, rows, lanes = array.shape
    return lax.all_to_all(
        array.reshape(n * rows, lanes), axis, split_axis=0, concat_axis=0, tiled=True
    ).reshape(n, rows, lanes)


def per_device(tile_vals, tile_rows, tile_cols, tile_count, start_panel):
    values = tile_vals[0, 0]
    slots = values.shape[0]
    n_group, n_loop = lax.axis_size("group"), lax.axis_size("loop")
    rows_dev, cols_dev = 2048, 2048
    row_blocks, col_blocks = rows_dev // SIDE, cols_dev // SIDE
    row_half, col_half = rows_dev // n_loop // 2, cols_dev // n_group // 2
    half = SIDE // 2

    alive = jnp.arange(slots) < tile_count[0, 0]
    row_from, col_from = tile_rows[0, 0], tile_cols[0, 0]
    row_to = jnp.where(alive, row_from, row_blocks)
    col_to = jnp.where(alive, col_from, col_blocks)

    col_part, row_part = call(
        degree_kernel,
        "degrees",
        [SMEM, SMEM, VMEM],
        [((col_blocks, SIDE), F32), ((row_blocks, SIDE), F32)],
        [pltpu.VMEM((col_blocks + 1, 8, SIDE), F32), pltpu.VMEM((row_blocks + 1, 8, SIDE), F32)],
    )(row_to, col_to, values)

    start = start_panel[0]
    start = jnp.concatenate([start[:col_half], start[col_half:]], axis=1)
    first = jnp.concatenate([start, col_part], axis=0)
    gathered = exchange(jnp.broadcast_to(first[None], (n_group,) + first.shape), "group")

    forward = values.reshape(slots, half // row_half, 2, row_half, SIDE)
    forward = forward.transpose(0, 1, 3, 2, 4).reshape(slots, half, 2 * SIDE)
    turned = values.transpose(0, 2, 1).reshape(slots, SIDE, half // row_half, 2, row_half)
    turned = turned.transpose(0, 1, 3, 2, 4).reshape(slots, half // col_half, 2, col_half, SIDE)
    backward = turned.transpose(0, 1, 3, 2, 4).reshape(slots, half, 2 * SIDE)

    pieces = row_part.reshape(n_loop, 2 * row_half)
    high = pieces.astype(BF16)
    middle = (pieces - high.astype(F32)).astype(BF16)
    low = (pieces - high.astype(F32) - middle.astype(F32)).astype(BF16)
    degrees = jnp.stack([high, middle, low], axis=1)
    degrees = jnp.pad(degrees, ((0, 0), (0, DEGREE_ROWS - 3), (0, LANES - 2 * row_half)))

    spread = lambda blocks: [
        pltpu.VMEM((blocks, 2 * SIDE, LANES), BF16),
    ]
    total = lambda blocks: [pltpu.VMEM((blocks + 1, half, LANES), F32)]

    col_scale = row_scale = col_weight = row_weight = None
    for iteration in range(ITERS):
        if iteration == 0:
            outgoing, col_weight = call(
                functools.partial(product_kernel, "start", n_group, col_half, n_loop, row_half),
                "forward_start",
                [SMEM, SMEM, VMEM, VMEM, VMEM],
                [((n_loop, row_half + DEGREE_ROWS, LANES), BF16), ((cols_dev // 2, LANES), F32)],
                spread(col_blocks) + total(row_blocks),
            )(col_from, row_to, gathered, forward, degrees)
            own = lax.axis_index("group") * col_half
            col_scale = lax.rsqrt(lax.dynamic_slice_in_dim(col_weight, own, col_half, 0))
        else:
            (outgoing,) = call(
                functools.partial(product_kernel, "plain", n_group, col_half, n_loop, row_half),
                "forward",
                [SMEM, SMEM, VMEM, VMEM, VMEM],
                [((n_loop, row_half + GRAM_ROWS, LANES), BF16)],
                spread(col_blocks) + total(row_blocks),
            )(col_from, row_to, gathered, forward, col_weight)
        received = exchange(outgoing, "loop")
        if iteration == 0:
            copies, attendee_sum, row_scale = call(
                functools.partial(sum_kernel, "degree", n_loop, row_half, n_loop),
                "attendee_start",
                [VMEM],
                [
                    ((n_loop, row_half + DEGREE_ROWS, LANES), BF16),
                    ((row_half, LANES), F32),
                    ((row_half, LANES), F32),
                ],
            )(received)
        else:
            copies, attendee_sum = call(
                functools.partial(sum_kernel, "plain", n_loop, row_half, n_loop),
                "attendee",
                [VMEM, VMEM],
                [((n_loop, row_half, LANES), BF16), ((row_half, LANES), F32)],
            )(received, row_scale)
        gathered = exchange(copies, "loop")
        if iteration == 0:
            outgoing, row_weight = call(
                functools.partial(product_kernel, "degree", n_loop, row_half, n_group, col_half),
                "backward_start",
                [SMEM, SMEM, VMEM, VMEM],
                [((n_group, col_half + GRAM_ROWS, LANES), BF16), ((rows_dev // 2, LANES), F32)],
                spread(row_blocks) + total(col_blocks),
            )(row_from, col_to, gathered, backward)
        else:
            (outgoing,) = call(
                functools.partial(product_kernel, "plain", n_loop, row_half, n_group, col_half),
                "backward",
                [SMEM, SMEM, VMEM, VMEM, VMEM],
                [((n_group, col_half + GRAM_ROWS, LANES), BF16)],
                spread(row_blocks) + total(col_blocks),
            )(row_from, col_to, gathered, backward, row_weight)
        received = exchange(outgoing, "group")
        if iteration < ITERS - 1:
            copies, session_sum = call(
                functools.partial(sum_kernel, "plain", n_group, col_half, n_group),
                "session",
                [VMEM, VMEM],
                [((n_group, col_half, LANES), BF16), ((col_half, LANES), F32)],
            )(received, col_scale)
            gathered = exchange(copies, "group")
        else:
            copies, session_sum, attendee = call(
                functools.partial(sum_kernel, "last", n_group, col_half, n_group),
                "session_last",
                [VMEM, VMEM, VMEM],
                [
                    ((n_group, WIDTH // 2, LANES), F32),
                    ((col_half, LANES), F32),
                    ((2 * row_half, WIDTH), F32),
                ],
            )(received, col_scale, attendee_sum)
    gram = jnp.sum(exchange(copies, "group"), axis=0)
    grams = exchange(jnp.broadcast_to(gram[None], (n_loop,) + gram.shape), "loop")
    (session,) = call(
        functools.partial(last_kernel, n_loop),
        "session_out",
        [VMEM, VMEM],
        [((2 * col_half, WIDTH), F32)],
    )(grams, session_sum)
    return (session[None], attendee[None])


def solution(mesh):
    in_specs = (
        P("group", "loop", None, None, None),
        P("group", "loop", None),
        P("group", "loop", None),
        P("group", "loop"),
        P("loop", "group", None),
    )
    out_specs = (P("loop", "group", None), P("group", "loop", None))
    return jax.shard_map(
        per_device, mesh=mesh, in_specs=in_specs, out_specs=out_specs, check_vma=False
    )
```

```python
import functools

import jax
import jax.numpy as jnp
from jax import lax
from jax.experimental import pallas as pl
from jax.experimental.pallas import tpu as pltpu
from jax.sharding import PartitionSpec as P

ITERS = 3
SIDE = 128
WIDTH = 64
LANES = 128
GRAM_ROWS = 48
DEGREE_ROWS = 16
F32 = jnp.float32
BF16 = jnp.bfloat16
HIGHEST = lax.Precision.HIGHEST


def iota(shape, dim):
    return lax.broadcasted_iota(jnp.int32, shape, dim)


def halves_to_rows(packed):
    return jnp.concatenate([packed[:, :WIDTH], packed[:, WIDTH:]], axis=0)


def rows_to_halves(rows):
    half = rows.shape[0] // 2
    return jnp.concatenate([rows[:half], rows[half:]], axis=1)


def lanes_to_packed(row, half):
    shape = (half, LANES)
    spread = jnp.broadcast_to(row, shape)
    delta = iota(shape, 1) - iota(shape, 0)
    first = jnp.sum(jnp.where(delta == 0, spread, 0.0), axis=1, keepdims=True)
    last = jnp.sum(jnp.where(delta == half, spread, 0.0), axis=1, keepdims=True)
    return jnp.where(iota(shape, 1) < WIDTH, first, last)


def split_two(value):
    high = value.astype(BF16).astype(F32)
    return high, value - high


def diagonal_blocks(square):
    return square[:WIDTH, :WIDTH] + square[WIDTH:, WIDTH:]


def inverse_factor(gram):
    shape = (WIDTH, WIDTH)
    on_diagonal = iota(shape, 0) == iota(shape, 1)
    diagonal = jnp.where(on_diagonal, gram, 0.0)
    down = lax.rsqrt(jnp.sum(diagonal, axis=1, keepdims=True))
    across = lax.rsqrt(jnp.sum(diagonal, axis=0, keepdims=True))
    whole = jnp.concatenate([gram * down * across, jnp.where(on_diagonal, 1.0, 0.0)], axis=1)
    n_blocks = WIDTH // 8
    blocks = [whole[8 * b : 8 * b + 8] for b in range(n_blocks)]
    below = iota((8, LANES), 0)
    for p in range(n_blocks):
        spread = {
            b: [
                jnp.broadcast_to(blocks[b][:, 8 * p + j : 8 * p + j + 1], (8, LANES))
                for j in range(8)
            ]
            for b in range(p, n_blocks)
        }
        for k in range(0, 8, 2):
            own = list(spread[p])
            p00, p01, p11 = own[k][k : k + 1], own[k + 1][k : k + 1], own[k + 1][k + 1 : k + 2]
            inverse = 1.0 / (p00 * p11 - p01 * p01)
            q00, q01, q11 = p11 * inverse, p01 * inverse, p00 * inverse
            row0, row1 = blocks[p][k : k + 1], blocks[p][k + 1 : k + 2]
            for b in range(p, n_blocks):
                if b == p and k == 6:
                    continue
                column0, column1 = spread[b][k], spread[b][k + 1]
                if b == p:
                    column0 = jnp.where(below > k + 1, column0, 0.0)
                    column1 = jnp.where(below > k + 1, column1, 0.0)
                times0 = q00 * column0 - q01 * column1
                times1 = q11 * column1 - q01 * column0
                for j in range(k + 2, 8):
                    spread[b][j] = spread[b][j] - (
                        times0 * own[j][k : k + 1] + times1 * own[j][k + 1 : k + 2]
                    )
                blocks[b] = blocks[b] - (times0 * row0 + times1 * row1)
    whole = jnp.concatenate(blocks, axis=0)
    left, right = whole[:, :WIDTH], whole[:, WIDTH:]
    pivots = jnp.sum(jnp.where(on_diagonal, left, 0.0), axis=1, keepdims=True)
    beside = iota(shape, 0) == iota(shape, 1) + 1
    coupling = jnp.sum(jnp.where(beside, left, 0.0), axis=1, keepdims=True)
    above = jnp.concatenate([pivots[WIDTH - 1 :], pivots[: WIDTH - 1]], axis=0)
    right_above = jnp.concatenate([right[WIDTH - 1 :], right[: WIDTH - 1]], axis=0)
    odd = iota((WIDTH, 1), 0) % 2 == 1
    ratio = jnp.where(odd, coupling / above, 0.0)
    return (right - ratio * right_above) * lax.rsqrt(pivots - ratio * coupling) * across


def both_halves(inverse):
    zero = jnp.zeros((WIDTH, WIDTH), F32)
    return jnp.concatenate(
        [
            jnp.concatenate([inverse, zero], axis=1),
            jnp.concatenate([zero, inverse], axis=1),
        ],
        axis=0,
    )


def times_transposed(left, right):
    return lax.dot_general(
        left, right, (((1,), (1,)), ((), ())), precision=HIGHEST, preferred_element_type=F32
    )


def factor_parts(both):
    high, low = split_two(both.T)
    return jnp.concatenate([high, high, low], axis=0).astype(BF16)


def apply_to_gram(gram, inverse):
    turned = jnp.dot(inverse, gram, precision=HIGHEST, preferred_element_type=F32)
    return times_transposed(turned, inverse)


def gram_to_message(gram, whole):
    shape = (WIDTH, WIDTH)
    on_diagonal = iota(shape, 0) == iota(shape, 1)
    high, low = split_two(gram)
    mixed = jnp.where(iota(shape, 0) >= iota(shape, 1), high, low.T)
    if not whole:
        mixed = jnp.where(on_diagonal, gram * (1.0 + 2.0**-7), mixed)
    message = rows_to_halves(mixed)
    if whole:
        diagonal = jnp.sum(jnp.where(on_diagonal, low, 0.0), axis=0, keepdims=True)
        diagonal = jnp.concatenate([diagonal, diagonal], axis=1)
        message = jnp.concatenate([message, jnp.broadcast_to(diagonal, (16, LANES))], axis=0)
    return message.astype(BF16)


def message_to_gram(message):
    shape = (WIDTH, WIDTH)
    square = halves_to_rows(message[:32])
    on_diagonal = iota(shape, 0) == iota(shape, 1)
    whole = square if message.shape[0] == 32 else square + message[32:33, :WIDTH]
    return jnp.where(on_diagonal, whole, square + square.T)


def degree_kernel(count, row_at, col_at, values, start, copies, row_degree, col_sum, row_sum):
    n_blocks = row_degree.shape[0]
    col_sum[...] = jnp.zeros_like(col_sum)
    row_sum[...] = jnp.zeros_like(row_sum)
    ones = jnp.ones((8, SIDE), BF16)
    for t in range(values.shape[0]):
        tile = values[t]
        alive = t < count[0]
        col_sum[jnp.where(alive, col_at[t], n_blocks)] += jnp.dot(
            ones, tile, preferred_element_type=F32
        )
        row_sum[jnp.where(alive, row_at[t], n_blocks)] += lax.dot_general(
            ones, tile, (((1,), (1,)), ((), ())), preferred_element_type=F32
        )
    for b in range(n_blocks):
        row_degree[b : b + 1] = row_sum[b, :1]
    panel = rows_to_halves(start[...].T)
    degree = jnp.concatenate([col_sum[b, :1] for b in range(n_blocks)], axis=0)
    for d in range(copies.shape[0]):
        copies[d, : panel.shape[0]] = panel
        copies[d, panel.shape[0] :] = degree


def layout_kernel(row_half, col_half, values, forward, backward):
    half = SIDE // 2
    slabs = [slice(at, at + row_half) for at in range(0, SIDE, row_half)]
    for t in range(values.shape[0]):
        tile = values[t]
        for at in range(0, half, row_half):
            forward[t, at : at + row_half, :SIDE] = tile[2 * at : 2 * at + row_half]
            forward[t, at : at + row_half, SIDE:] = tile[2 * at + row_half : 2 * at + 2 * row_half]
        order = slabs[0::2] + slabs[1::2]
        turned = jnp.concatenate([tile[rows] for rows in order], axis=0).T
        for at in range(0, half, col_half):
            backward[t, at : at + col_half, :SIDE] = turned[2 * at : 2 * at + col_half]
            backward[t, at : at + col_half, SIDE:] = turned[2 * at + col_half : 2 * at + 2 * col_half]


def product_kernel(kind, rows_from, n_to, rows_to, whole, *refs):
    count, source, target, gathered, tiles = refs[:5]
    if kind == "start":
        row_degree, out, weight, own_scale, spread, total = refs[5:]
    elif kind == "degree":
        out, weight, spread, total = refs[5:]
    elif whole:
        weight, factor, pending, out, spread, total = refs[5:]
    else:
        weight, factor, out, spread, total = refs[5:]
    half = SIDE // 2
    lane_low = iota((half, LANES), 1) < WIDTH
    n_blocks = total.shape[0] - 1
    per_block = half // rows_from

    if kind == "start":
        degree = 1.0 + jnp.sum(gathered[:, rows_from:, :], axis=0)

    grams = jnp.zeros((2 * LANES, LANES), F32)
    for b in range(n_blocks):
        rows = slice(b * half, (b + 1) * half)
        if kind == "start":
            packed_degree = lanes_to_packed(degree[b : b + 1], half)
            weight[rows] = packed_degree
            panel = (gathered[b, :rows_from] * lax.rsqrt(packed_degree)).astype(BF16).astype(F32)
        else:
            parts = [
                gathered[b * per_block + j, :rows_from].astype(F32) for j in range(per_block)
            ]
            panel = parts[0] if per_block == 1 else jnp.concatenate(parts, axis=0)
        if kind == "degree":
            packs = []
            for j in range(per_block):
                pieces = gathered[b * per_block + j, rows_from:].astype(F32)
                packs.append(lanes_to_packed(jnp.sum(pieces[:3], axis=0, keepdims=True), rows_from))
            packed_degree = packs[0] if per_block == 1 else jnp.concatenate(packs, axis=0)
            weight[rows] = packed_degree
        turned = pltpu.roll(panel, WIDTH, 1)
        spread[b, :half] = jnp.where(lane_low, panel, 0.0).astype(BF16)
        spread[b, half : 2 * half] = jnp.where(lane_low, turned, 0.0).astype(BF16)
        spread[b, 2 * half : 3 * half] = jnp.where(lane_low, 0.0, turned).astype(BF16)
        spread[b, 3 * half :] = jnp.where(lane_low, 0.0, panel).astype(BF16)
        if kind != "start":
            high, low = split_two(panel * weight[rows])
            both = jnp.concatenate([high, low], axis=1).astype(BF16)
            grams = grams + lax.dot_general(
                both, panel.astype(BF16), (((0,), (0,)), ((), ())), preferred_element_type=F32
            )
        total[b] = jnp.zeros((half, LANES), F32)
    total[n_blocks] = jnp.zeros((half, LANES), F32)

    for t in range(tiles.shape[0]):
        at = jnp.where(t < count[0], target[t], n_blocks)
        total[at] += jnp.dot(tiles[t], spread[source[t]], preferred_element_type=F32)

    if kind == "start":
        degrees = row_degree[...]
        parts = []
        for value in (degrees, pltpu.roll(degrees, WIDTH, 1)):
            high, rest = split_two(value)
            parts.append((high, *split_two(rest)))
        at = iota((DEGREE_ROWS, LANES), 0)
    else:
        gram = diagonal_blocks(grams[:LANES]) + diagonal_blocks(grams[LANES:])
        if whole:
            gram = apply_to_gram(gram, pending[:WIDTH, :WIDTH])
        message = gram_to_message(gram, whole)
    if kind == "start":
        own = lax.axis_index("group")
        own_scale[...] = lax.rsqrt(weight[pl.ds(own * rows_from, rows_from)])
    to_block = half // rows_to
    for b in range(n_blocks):
        product = total[b]
        if kind == "plain":
            high, low = split_two(product)
            mixed = jnp.concatenate([high, low, high], axis=1).astype(BF16)
            product = jnp.dot(mixed, factor[...], preferred_element_type=F32)
        product = product.astype(BF16)
        for j in range(to_block):
            d = b * to_block + j
            out[d, :rows_to] = product[j * rows_to : (j + 1) * rows_to]
            if kind == "start":
                high, middle, low = (part[b : b + 1] for part in parts[j])
                tail = jnp.where(at == 0, high, jnp.where(at == 1, middle, low))
                out[d, rows_to:] = jnp.where(at < 3, tail, 0.0).astype(BF16)
            else:
                out[d, rows_to:] = message


def sum_kernel(kind, n_from, rows, n_copies, *refs):
    if kind == "degree":
        received, copies, panel_out, scale_out = refs
    else:
        received, scale_ref, copies, panel_out, gram_out = refs
    summed = received[0].astype(F32)
    for s in range(1, n_from):
        summed = summed + received[s].astype(F32)
    panel = summed[:rows]
    if kind == "degree":
        degree = 1.0 + jnp.sum(summed[rows : rows + 3], axis=0, keepdims=True)
        scale = lax.rsqrt(lanes_to_packed(degree, rows))
        scale_out[...] = scale
    else:
        scale = scale_ref[...]
        gram_out[...] = message_to_gram(summed[rows:])
    panel = panel * scale
    panel_out[...] = panel
    if kind == "last":
        square = lax.dot_general(
            panel, panel, (((0,), (0,)), ((), ())), precision=HIGHEST, preferred_element_type=F32
        )
        message = rows_to_halves(diagonal_blocks(square))
    else:
        message = (panel * scale).astype(BF16)
    for d in range(n_copies):
        copies[d, : message.shape[0]] = message
    if kind == "degree":
        high, rest = split_two(degree)
        middle, low = split_two(rest)
        at = iota((DEGREE_ROWS, LANES), 0)
        tail = jnp.where(at == 0, high, jnp.where(at == 1, middle, jnp.where(at == 2, low, 0.0)))
        tail = tail.astype(BF16)
        for d in range(n_copies):
            copies[d, rows:] = tail


def factor_kernel(*refs):
    gram_ref, *pending, factor, parts = refs
    gram = gram_ref[...]
    if pending:
        gram = apply_to_gram(gram, pending[0][:WIDTH, :WIDTH])
    both = both_halves(inverse_factor(gram))
    factor[...] = both
    parts[...] = factor_parts(both)


def factor_last_kernel(gram, session, attendee, attendee_factor, factor, session_out, attendee_out):
    both = both_halves(inverse_factor(gram[...]))
    factor[...] = both
    session_out[...] = times_transposed(session[...], both)
    turned = times_transposed(attendee[...], attendee_factor[...])
    attendee_out[...] = halves_to_rows(times_transposed(turned, both))


def gram_last_kernel(n_from, n_copies, received, factor, copies):
    summed = received[0]
    for s in range(1, n_from):
        summed = summed + received[s]
    gram = apply_to_gram(halves_to_rows(summed), factor[:WIDTH, :WIDTH])
    message = gram_to_message(gram, True)
    for d in range(n_copies):
        copies[d] = message


def last_kernel(n_from, received, panel, out):
    summed = received[0].astype(F32)
    for s in range(1, n_from):
        summed = summed + received[s].astype(F32)
    both = both_halves(inverse_factor(message_to_gram(summed)))
    out[...] = halves_to_rows(times_transposed(panel[...], both)).T


VMEM = pl.BlockSpec(memory_space=pltpu.VMEM)
SMEM = pl.BlockSpec(memory_space=pltpu.SMEM)


def call(kernel, name, in_specs, out_shapes, scratch=(), flops=10**8, in_hbm=()):
    return pl.pallas_call(
        kernel,
        name=name,
        in_specs=in_specs,
        out_specs=[VMEM] * len(out_shapes),
        out_shape=[
            pltpu.HBM(s, d) if i in in_hbm else jax.ShapeDtypeStruct(s, d)
            for i, (s, d) in enumerate(out_shapes)
        ],
        scratch_shapes=list(scratch),
        cost_estimate=pl.CostEstimate(flops=flops, bytes_accessed=2**20, transcendentals=0),
        compiler_params=pltpu.CompilerParams(vmem_limit_bytes=32 * 1024 * 1024),
    )


def from_hbm(*arrays):
    return [pltpu.with_memory_space_constraint(array, pltpu.HBM) for array in arrays]


def exchange(array, axis):
    n, rows, lanes = array.shape
    return lax.all_to_all(
        array.reshape(n * rows, lanes), axis, split_axis=0, concat_axis=0, tiled=True
    ).reshape(n, rows, lanes)


def per_device(tile_vals, tile_rows, tile_cols, tile_count, start_panel):
    values = tile_vals[0, 0]
    slots = values.shape[0]
    n_group, n_loop = lax.axis_size("group"), lax.axis_size("loop")
    rows_dev, cols_dev = 2048, 2048
    row_blocks, col_blocks = rows_dev // SIDE, cols_dev // SIDE
    row_half, col_half = rows_dev // n_loop // 2, cols_dev // n_group // 2
    half = SIDE // 2
    count, row_at, col_at = tile_count[0], tile_rows[0, 0], tile_cols[0, 0]

    first, row_degree = call(
        degree_kernel,
        "degrees",
        [SMEM, SMEM, SMEM, VMEM, VMEM],
        [((n_group, col_half + col_blocks, LANES), F32), ((row_blocks, SIDE), F32)],
        [pltpu.VMEM((col_blocks + 1, 8, SIDE), F32), pltpu.VMEM((row_blocks + 1, 8, SIDE), F32)],
    )(count, row_at, col_at, values, start_panel[0].T)
    gathered = exchange(first, "group")
    forward, backward = call(
        functools.partial(layout_kernel, row_half, col_half),
        "layouts",
        [VMEM],
        [((slots, half, 2 * SIDE), BF16), ((slots, half, 2 * SIDE), BF16)],
    )(values)

    def scratch(blocks_from, blocks_to):
        return [
            pltpu.VMEM((blocks_from, 2 * SIDE, LANES), BF16),
            pltpu.VMEM((blocks_to + 1, half, LANES), F32),
        ]

    def factor_of(*args):
        return call(
            factor_kernel,
            "factor",
            [VMEM] * len(args),
            [((LANES, LANES), F32), ((3 * LANES, LANES), BF16)],
            in_hbm=(0,),
        )(*from_hbm(*args))

    def products(kind, whole, rows_from, n_to, rows_to, name, extra_rows, args, others=()):
        return call(
            functools.partial(product_kernel, kind, rows_from, n_to, rows_to, whole),
            name,
            [SMEM] * 3 + [VMEM] * (len(args) - 3),
            [((n_to, rows_to + extra_rows, LANES), BF16), *others],
            scratch(row_blocks, col_blocks),
        )(*args)

    gram_shape, panel_rows = ((WIDTH, WIDTH), F32), ((row_half, LANES), F32)
    panel_cols = ((col_half, LANES), F32)
    for iteration in range(ITERS):
        last = iteration == ITERS - 1
        args = (count, col_at, row_at, gathered, forward)
        to = (col_half, n_loop, row_half)
        if iteration == 0:
            outgoing, col_weight, col_scale = products(
                "start",
                False,
                *to,
                "forward_start",
                DEGREE_ROWS,
                (*args, row_degree),
                [((cols_dev // 2, LANES), F32), panel_cols],
            )
            received = exchange(outgoing, "loop")
            copies, attendee, row_scale = call(
                functools.partial(sum_kernel, "degree", n_loop, row_half, n_loop),
                "attendee_start",
                [VMEM],
                [((n_loop, row_half + DEGREE_ROWS, LANES), BF16), panel_rows, panel_rows],
            )(received)
        else:
            (outgoing,) = products(
                "plain", False, *to, "forward", 32, (*args, col_weight, col_parts)
            )
            received = exchange(outgoing, "loop")
            copies, attendee, gram = call(
                functools.partial(sum_kernel, "plain", n_loop, row_half, n_loop),
                "attendee",
                [VMEM, VMEM],
                [((n_loop, row_half, LANES), BF16), panel_rows, gram_shape],
                in_hbm=(0, 2),
            )(received, row_scale)
            row_factor, row_parts = factor_of(gram, col_factor)
        gathered = exchange(copies, "loop")
        args = (count, row_at, col_at, gathered, backward)
        to = (row_half, n_group, col_half)
        if iteration == 0:
            outgoing, row_weight = products(
                "degree", False, *to, "backward_start", 32, args, [((rows_dev // 2, LANES), F32)]
            )
        else:
            args = (*args, row_weight, row_parts)
            if last:
                args = (*args, *from_hbm(row_factor))
            (outgoing,) = products("plain", last, *to, "backward", 48 if last else 32, args)
        received = exchange(outgoing, "group")
        message = ((n_group, WIDTH // 2, LANES), F32) if last else ((n_group, col_half, LANES), BF16)
        copies, session, gram = call(
            functools.partial(sum_kernel, "last" if last else "plain", n_group, col_half, n_group),
            "session",
            [VMEM, VMEM],
            [message, panel_cols, gram_shape],
            in_hbm=(0, 2),
        )(received, col_scale)
        gathered = exchange(copies, "group")
        if iteration == 0:
            col_factor, col_parts = factor_of(gram)
        elif not last:
            col_factor, col_parts = factor_of(gram, row_factor)
    col_factor, session, attendee = call(
        factor_last_kernel,
        "factor_last",
        [VMEM] * 4,
        [((LANES, LANES), F32), panel_cols, ((2 * row_half, WIDTH), F32)],
    )(gram, session, attendee, row_factor)
    (copies,) = call(
        functools.partial(gram_last_kernel, n_group, n_loop),
        "gram_last",
        [VMEM, VMEM],
        [((n_loop, 48, LANES), BF16)],
    )(gathered, col_factor)
    (session,) = call(
        functools.partial(last_kernel, n_loop),
        "session_out",
        [VMEM, VMEM],
        [((WIDTH, 2 * col_half), F32)],
    )(exchange(copies, "loop"), session)
    return (session.T[None], attendee[None])


def solution(mesh):
    in_specs = (
        P("group", "loop", None, None, None),
        P("group", "loop", None),
        P("group", "loop", None),
        P("group", "loop"),
        P("loop", "group", None),
    )
    out_specs = (P("loop", "group", None), P("group", "loop", None))
    return jax.shard_map(
        per_device, mesh=mesh, in_specs=in_specs, out_specs=out_specs, check_vma=False
    )
```

```python
import functools

import jax
import jax.numpy as jnp
from jax import lax
from jax.experimental import pallas as pl
from jax.experimental.pallas import tpu as pltpu
from jax.sharding import PartitionSpec as P

ITERS = 3
SIDE = 128
WIDTH = 64
LANES = 128
GRAM_ROWS = 48
DEGREE_ROWS = 16
F32 = jnp.float32
BF16 = jnp.bfloat16
HIGHEST = lax.Precision.HIGHEST

LOOP_ORDER = [k % 8 * 4 + k // 8 for k in range(32)]
LOOP_PLACE = [LOOP_ORDER.index(at) for at in range(32)]


def iota(shape, dim):
    return lax.broadcasted_iota(jnp.int32, shape, dim)


def halves_to_rows(packed):
    return jnp.concatenate([packed[:, :WIDTH], packed[:, WIDTH:]], axis=0)


def rows_to_halves(rows):
    half = rows.shape[0] // 2
    return jnp.concatenate([rows[:half], rows[half:]], axis=1)


def lanes_to_packed(row, half):
    shape = (half, LANES)
    spread = jnp.broadcast_to(row, shape)
    delta = iota(shape, 1) - iota(shape, 0)
    first = jnp.sum(jnp.where(delta == 0, spread, 0.0), axis=1, keepdims=True)
    last = jnp.sum(jnp.where(delta == half, spread, 0.0), axis=1, keepdims=True)
    return jnp.where(iota(shape, 1) < WIDTH, first, last)


def split_two(value):
    high = value.astype(BF16).astype(F32)
    return high, value - high


def diagonal_blocks(square):
    return square[:WIDTH, :WIDTH] + square[WIDTH:, WIDTH:]


def inverse_factor(gram):
    shape = (WIDTH, WIDTH)
    on_diagonal = iota(shape, 0) == iota(shape, 1)
    diagonal = jnp.where(on_diagonal, gram, 0.0)
    down = lax.rsqrt(jnp.sum(diagonal, axis=1, keepdims=True))
    across = lax.rsqrt(jnp.sum(diagonal, axis=0, keepdims=True))
    whole = jnp.concatenate([gram * down * across, jnp.where(on_diagonal, 1.0, 0.0)], axis=1)
    n_blocks = WIDTH // 8
    blocks = [whole[8 * b : 8 * b + 8] for b in range(n_blocks)]
    below = iota((8, LANES), 0)
    for p in range(n_blocks):
        spread = {
            b: [
                jnp.broadcast_to(blocks[b][:, 8 * p + j : 8 * p + j + 1], (8, LANES))
                for j in range(8)
            ]
            for b in range(p, n_blocks)
        }
        for k in range(0, 8, 2):
            own = list(spread[p])
            p00, p01, p11 = own[k][k : k + 1], own[k + 1][k : k + 1], own[k + 1][k + 1 : k + 2]
            inverse = 1.0 / (p00 * p11 - p01 * p01)
            q00, q01, q11 = p11 * inverse, p01 * inverse, p00 * inverse
            row0, row1 = blocks[p][k : k + 1], blocks[p][k + 1 : k + 2]
            for b in range(p, n_blocks):
                if b == p and k == 6:
                    continue
                column0, column1 = spread[b][k], spread[b][k + 1]
                if b == p:
                    column0 = jnp.where(below > k + 1, column0, 0.0)
                    column1 = jnp.where(below > k + 1, column1, 0.0)
                times0 = q00 * column0 - q01 * column1
                times1 = q11 * column1 - q01 * column0
                for j in range(k + 2, 8):
                    spread[b][j] = spread[b][j] - (
                        times0 * own[j][k : k + 1] + times1 * own[j][k + 1 : k + 2]
                    )
                blocks[b] = blocks[b] - (times0 * row0 + times1 * row1)
    whole = jnp.concatenate(blocks, axis=0)
    left, right = whole[:, :WIDTH], whole[:, WIDTH:]
    pivots = jnp.sum(jnp.where(on_diagonal, left, 0.0), axis=1, keepdims=True)
    beside = iota(shape, 0) == iota(shape, 1) + 1
    coupling = jnp.sum(jnp.where(beside, left, 0.0), axis=1, keepdims=True)
    above = jnp.concatenate([pivots[WIDTH - 1 :], pivots[: WIDTH - 1]], axis=0)
    right_above = jnp.concatenate([right[WIDTH - 1 :], right[: WIDTH - 1]], axis=0)
    odd = iota((WIDTH, 1), 0) % 2 == 1
    ratio = jnp.where(odd, coupling / above, 0.0)
    return (right - ratio * right_above) * lax.rsqrt(pivots - ratio * coupling) * across


def both_halves(inverse):
    zero = jnp.zeros((WIDTH, WIDTH), F32)
    return jnp.concatenate(
        [
            jnp.concatenate([inverse, zero], axis=1),
            jnp.concatenate([zero, inverse], axis=1),
        ],
        axis=0,
    )


def times_transposed(left, right):
    return lax.dot_general(
        left, right, (((1,), (1,)), ((), ())), precision=HIGHEST, preferred_element_type=F32
    )


def factor_parts(both):
    high, low = split_two(both.T)
    return jnp.concatenate([high, high, low], axis=0).astype(BF16)


def apply_to_gram(gram, inverse):
    turned = jnp.dot(inverse, gram, precision=HIGHEST, preferred_element_type=F32)
    return times_transposed(turned, inverse)


def gram_to_message(gram, whole):
    shape = (WIDTH, WIDTH)
    on_diagonal = iota(shape, 0) == iota(shape, 1)
    high, low = split_two(gram)
    mixed = jnp.where(iota(shape, 0) >= iota(shape, 1), high, low.T)
    if not whole:
        mixed = jnp.where(on_diagonal, gram * (1.0 + 2.0**-7), mixed)
    message = rows_to_halves(mixed)
    if whole:
        diagonal = jnp.sum(jnp.where(on_diagonal, low, 0.0), axis=0, keepdims=True)
        diagonal = jnp.concatenate([diagonal, diagonal], axis=1)
        message = jnp.concatenate([message, jnp.broadcast_to(diagonal, (16, LANES))], axis=0)
    return message.astype(BF16)


def message_to_gram(message):
    shape = (WIDTH, WIDTH)
    half = message.shape[0] // 2
    square = halves_to_rows(jnp.concatenate([message[:16], message[half : half + 16]], axis=0))
    on_diagonal = iota(shape, 0) == iota(shape, 1)
    whole = square if half == 16 else square + message[16:17, :WIDTH]
    return jnp.where(on_diagonal, whole, square + square.T)


def degree_kernel(count, row_at, col_at, values, start, copies, row_degree, col_sum, row_sum):
    n_blocks = row_degree.shape[0]
    col_sum[...] = jnp.zeros_like(col_sum)
    row_sum[...] = jnp.zeros_like(row_sum)
    ones = jnp.ones((8, SIDE), BF16)
    for t in range(values.shape[0]):
        tile = values[t]
        alive = t < count[0]
        col_sum[jnp.where(alive, col_at[t], n_blocks)] += jnp.dot(
            ones, tile, preferred_element_type=F32
        )
        row_sum[jnp.where(alive, row_at[t], n_blocks)] += lax.dot_general(
            ones, tile, (((1,), (1,)), ((), ())), preferred_element_type=F32
        )
    for b in range(n_blocks):
        row_degree[b : b + 1] = row_sum[b, :1]
    panel = rows_to_halves(start[...].T)
    degree = jnp.concatenate([col_sum[b, :1] for b in range(n_blocks)], axis=0)
    for d in range(copies.shape[0]):
        copies[d, : panel.shape[0]] = panel
        copies[d, panel.shape[0] :] = degree


def layout_kernel(row_half, col_half, values, forward, backward):
    half = SIDE // 2
    slabs = [slice(at, at + row_half) for at in range(0, SIDE, row_half)]
    for t in range(values.shape[0]):
        tile = values[t]
        for at in range(0, half, row_half):
            forward[t, at : at + row_half, :SIDE] = tile[2 * at : 2 * at + row_half]
            forward[t, at : at + row_half, SIDE:] = tile[2 * at + row_half : 2 * at + 2 * row_half]
        order = slabs[0::2] + slabs[1::2]
        turned = jnp.concatenate([tile[rows] for rows in order], axis=0).T
        for at in range(0, half, col_half):
            backward[t, at : at + col_half, :SIDE] = turned[2 * at : 2 * at + col_half]
            backward[t, at : at + col_half, SIDE:] = turned[2 * at + col_half : 2 * at + 2 * col_half]


def product_kernel(kind, source, target, rows_from, n_to, rows_to, whole, from_pair, *refs):
    index, gathered, tiles, *refs, spread, total = refs
    if kind == "start":
        row_degree, out, weight, own_scale = refs
    elif kind == "degree":
        out, weight = refs
    elif whole:
        weight, factor, pending, out = refs
    else:
        weight, factor, out = refs
    half = SIDE // 2
    lane_low = iota((half, LANES), 1) < WIDTH
    n_blocks = total.shape[0] - 1
    per_block = half // rows_from

    if kind == "start":
        degree = 1.0 + jnp.sum(gathered[:, rows_from:, :], axis=0)

    grams = jnp.zeros((2 * LANES, LANES), F32)
    for b in range(n_blocks):
        rows = slice(b * half, (b + 1) * half)
        if kind == "start":
            packed_degree = lanes_to_packed(degree[b : b + 1], half)
            weight[rows] = packed_degree
            place = b % 2 * (n_blocks // 2) + b // 2
            panel = gathered[place, :rows_from] * lax.rsqrt(packed_degree)
            panel = panel.astype(BF16).astype(F32)
        else:
            places = [b * per_block + j for j in range(per_block)]
            if per_block > 1:
                places = [LOOP_PLACE[place] for place in places]
            parts = [gathered[place, :rows_from].astype(F32) for place in places]
            panel = parts[0] if per_block == 1 else jnp.concatenate(parts, axis=0)
        if kind == "degree":
            packs = []
            for place in places:
                pieces = gathered[place, rows_from:].astype(F32)
                packs.append(lanes_to_packed(jnp.sum(pieces[:3], axis=0, keepdims=True), rows_from))
            packed_degree = packs[0] if per_block == 1 else jnp.concatenate(packs, axis=0)
            weight[rows] = packed_degree
        turned = pltpu.roll(panel, WIDTH, 1)
        spread[b, :half] = jnp.where(lane_low, panel, 0.0).astype(BF16)
        spread[b, half : 2 * half] = jnp.where(lane_low, turned, 0.0).astype(BF16)
        spread[b, 2 * half : 3 * half] = jnp.where(lane_low, 0.0, turned).astype(BF16)
        spread[b, 3 * half :] = jnp.where(lane_low, 0.0, panel).astype(BF16)
        if kind != "start":
            high, low = split_two(panel * weight[rows])
            both = jnp.concatenate([high, low], axis=1).astype(BF16)
            grams = grams + lax.dot_general(
                both, panel.astype(BF16), (((0,), (0,)), ((), ())), preferred_element_type=F32
            )
        total[b] = jnp.zeros((half, LANES), F32)
    total[n_blocks] = jnp.zeros((half, LANES), F32)

    for t in range(tiles.shape[0]):
        total[index[target, t]] += jnp.dot(
            tiles[t], spread[index[source, t]], preferred_element_type=F32
        )

    if kind == "start":
        degrees = row_degree[...]
        parts = []
        for value in (degrees, pltpu.roll(degrees, WIDTH, 1)):
            high, rest = split_two(value)
            parts.append((high, *split_two(rest)))
        at = iota((DEGREE_ROWS, LANES), 0)
    else:
        gram = diagonal_blocks(grams[:LANES]) + diagonal_blocks(grams[LANES:])
        if whole:
            gram = apply_to_gram(gram, pending[:WIDTH, :WIDTH])
        message = gram_to_message(gram, whole)
        halves = [message[:16], message[16:32]]
        if whole:
            halves = [jnp.concatenate([part, message[32:]], axis=0) for part in halves]
        if from_pair:
            halves = [jnp.where(index[4, 1] == 0, *halves)] * 2
    if kind == "start":
        own = index[4, 0]
        own_scale[...] = lax.rsqrt(weight[pl.ds(own * rows_from, rows_from)])
    to_block = half // rows_to
    for b in range(n_blocks):
        product = total[b]
        if kind == "plain":
            high, low = split_two(product)
            mixed = jnp.concatenate([high, low, high], axis=1).astype(BF16)
            product = jnp.dot(mixed, factor[...], preferred_element_type=F32)
        product = product.astype(BF16)
        for j in range(to_block):
            d = LOOP_PLACE[b * to_block + j] if to_block > 1 else b
            out[d, :rows_to] = product[j * rows_to : (j + 1) * rows_to]
            if kind == "start":
                high, middle, low = (part[b : b + 1] for part in parts[j])
                tail = jnp.where(at == 0, high, jnp.where(at == 1, middle, low))
                out[d, rows_to:] = jnp.where(at < 3, tail, 0.0).astype(BF16)
            else:
                out[d, rows_to:] = halves[b % 2]


def sum_kernel(kind, n_from, rows, n_copies, *refs):
    if kind == "degree":
        received, copies, panel_out, scale_out = refs
    else:
        received, scale_ref, copies, panel_out, gram_out = refs
    summed = received[0].astype(F32)
    for s in range(1, n_from):
        summed = summed + received[s].astype(F32)
    panel = summed[:rows]
    if kind == "degree":
        degree = 1.0 + jnp.sum(summed[rows : rows + 3], axis=0, keepdims=True)
        scale = lax.rsqrt(lanes_to_packed(degree, rows))
        scale_out[...] = scale
    else:
        scale = scale_ref[...]
        gram_out[...] = summed[rows:]
    panel = panel * scale
    panel_out[...] = panel
    if kind == "last":
        square = lax.dot_general(
            panel, panel, (((0,), (0,)), ((), ())), precision=HIGHEST, preferred_element_type=F32
        )
        message = rows_to_halves(diagonal_blocks(square))
    else:
        message = (panel * scale).astype(BF16)
    for d in range(n_copies):
        copies[d, : message.shape[0]] = message
    if kind == "degree":
        high, rest = split_two(degree)
        middle, low = split_two(rest)
        at = iota((DEGREE_ROWS, LANES), 0)
        tail = jnp.where(at == 0, high, jnp.where(at == 1, middle, jnp.where(at == 2, low, 0.0)))
        tail = tail.astype(BF16)
        for d in range(n_copies):
            copies[d, rows:] = tail


def factor_kernel(*refs):
    gram_ref, *pending, factor, parts = refs
    gram = message_to_gram(gram_ref[...])
    if pending:
        gram = apply_to_gram(gram, pending[0][:WIDTH, :WIDTH])
    both = both_halves(inverse_factor(gram))
    factor[...] = both
    parts[...] = factor_parts(both)


def factor_last_kernel(gram, session, attendee, attendee_factor, factor, session_out, attendee_out):
    both = both_halves(inverse_factor(message_to_gram(gram[...])))
    factor[...] = both
    session_out[...] = times_transposed(session[...], both)
    turned = times_transposed(attendee[...], attendee_factor[...])
    attendee_out[...] = halves_to_rows(times_transposed(turned, both))


def gram_last_kernel(n_from, n_copies, received, factor, copies):
    summed = received[0]
    for s in range(1, n_from):
        summed = summed + received[s]
    gram = apply_to_gram(halves_to_rows(summed), factor[:WIDTH, :WIDTH])
    message = gram_to_message(gram, True)
    for d in range(n_copies):
        copies[d] = message


def last_kernel(n_from, received, panel, out):
    summed = received[0].astype(F32)
    for s in range(1, n_from):
        summed = summed + received[s].astype(F32)
    message = jnp.concatenate([summed[:16], summed[32:], summed[16:]], axis=0)
    both = both_halves(inverse_factor(message_to_gram(message)))
    out[...] = halves_to_rows(times_transposed(panel[...], both)).T


VMEM = pl.BlockSpec(memory_space=pltpu.VMEM)
SMEM = pl.BlockSpec(memory_space=pltpu.SMEM)


def call(kernel, name, in_specs, out_shapes, scratch=(), flops=10**8, in_hbm=()):
    return pl.pallas_call(
        kernel,
        name=name,
        in_specs=in_specs,
        out_specs=[VMEM] * len(out_shapes),
        out_shape=[
            pltpu.HBM(s, d) if i in in_hbm else jax.ShapeDtypeStruct(s, d)
            for i, (s, d) in enumerate(out_shapes)
        ],
        scratch_shapes=list(scratch),
        cost_estimate=pl.CostEstimate(flops=flops, bytes_accessed=2**20, transcendentals=0),
        compiler_params=pltpu.CompilerParams(vmem_limit_bytes=32 * 1024 * 1024),
    )


def from_hbm(*arrays):
    return [pltpu.with_memory_space_constraint(array, pltpu.HBM) for array in arrays]


def exchange(array, axis, groups=None):
    n, rows, lanes = array.shape
    return lax.all_to_all(
        array.reshape(n * rows, lanes),
        axis,
        split_axis=0,
        concat_axis=0,
        axis_index_groups=groups or ([LOOP_ORDER] if axis == "loop" else None),
        tiled=True,
    ).reshape(n, rows, lanes)


def per_device(tile_vals, tile_rows, tile_cols, tile_count, start_panel):
    values = tile_vals[0, 0]
    slots = values.shape[0]
    n_group, n_loop = lax.axis_size("group"), lax.axis_size("loop")
    rows_dev, cols_dev = 2048, 2048
    row_blocks, col_blocks = rows_dev // SIDE, cols_dev // SIDE
    row_half, col_half = rows_dev // n_loop // 2, cols_dev // n_group // 2
    half = SIDE // 2
    count, row_at, col_at = tile_count[0], tile_rows[0, 0], tile_cols[0, 0]

    first, row_degree = call(
        degree_kernel,
        "degrees",
        [SMEM, SMEM, SMEM, VMEM, VMEM],
        [((n_group // 2, col_half + col_blocks, LANES), F32), ((row_blocks, SIDE), F32)],
        [pltpu.VMEM((col_blocks + 1, 8, SIDE), F32), pltpu.VMEM((row_blocks + 1, 8, SIDE), F32)],
    )(count, row_at, col_at, *from_hbm(values, start_panel[0].T))
    pairs = [[i, i + 1] for i in range(0, n_group, 2)]
    gathered = exchange(first, "group", [list(range(core, n_group, 2)) for core in range(2)])
    gathered = lax.all_gather(gathered, "group", axis_index_groups=pairs, axis=0, tiled=True)
    forward, backward = call(
        functools.partial(layout_kernel, row_half, col_half),
        "layouts",
        [VMEM],
        [((slots, half, 2 * SIDE), BF16), ((slots, half, 2 * SIDE), BF16)],
    )(values)

    alive = jnp.arange(slots) < count
    group = lax.axis_index("group")
    index = [row_at, col_at, jnp.where(alive, row_at, row_blocks)]
    index += [jnp.where(alive, col_at, col_blocks), jnp.pad(jnp.stack([group, group % 2]), (0, slots - 2))]
    index = jnp.pad(jnp.stack(index).astype(jnp.int32), ((0, 3), (0, LANES - slots)))
    scratch = [
        pltpu.VMEM((col_blocks, 2 * SIDE, LANES), BF16),
        pltpu.VMEM((row_blocks + 1, half, LANES), F32),
    ]

    def factor_of(*args):
        return call(
            factor_kernel,
            "factor",
            [VMEM] * len(args),
            [((LANES, LANES), F32), ((3 * LANES, LANES), BF16)],
            in_hbm=(0,),
        )(*from_hbm(*args))

    def products(kind, way, whole, rows_from, n_to, rows_to, name, extra_rows, args, others=()):
        return call(
            functools.partial(
                product_kernel, kind, *way, rows_from, n_to, rows_to, whole, n_to == n_loop
            ),
            name,
            [SMEM] + [VMEM] * len(args),
            [((n_to, rows_to + extra_rows, LANES), BF16), *others],
            scratch,
        )(index, *args)

    def swap_cores(half_message):
        return lax.all_gather(
            half_message, "group", axis_index_groups=pairs, axis=0, tiled=True
        )

    panel_rows = ((row_half, LANES), F32)
    panel_cols = ((col_half, LANES), F32)
    for iteration in range(ITERS):
        last = iteration == ITERS - 1
        args = (gathered, forward)
        to = (col_half, n_loop, row_half)
        if iteration == 0:
            outgoing, col_weight, col_scale = products(
                "start",
                (1, 2),
                False,
                *to,
                "forward_start",
                DEGREE_ROWS,
                (*args, row_degree),
                [((cols_dev // 2, LANES), F32), panel_cols],
            )
            received = exchange(outgoing, "loop")
            copies, attendee, row_scale = call(
                functools.partial(sum_kernel, "degree", n_loop, row_half, n_loop),
                "attendee_start",
                [VMEM],
                [((n_loop, row_half + DEGREE_ROWS, LANES), BF16), panel_rows, panel_rows],
            )(received)
        else:
            (outgoing,) = products(
                "plain", (1, 2), False, *to, "forward", 16, (*args, col_weight, col_parts)
            )
            received = exchange(outgoing, "loop")
            copies, attendee, gram = call(
                functools.partial(sum_kernel, "plain", n_loop, row_half, n_loop),
                "attendee",
                [VMEM, VMEM],
                [((n_loop, row_half, LANES), BF16), panel_rows, ((16, LANES), F32)],
                in_hbm=(0, 2),
            )(received, row_scale)
            row_factor, row_parts = factor_of(swap_cores(gram), col_factor)
        gathered = exchange(copies, "loop")
        args = (gathered, backward)
        to = (row_half, n_group, col_half)
        message_rows = 32 if last else 16
        if iteration == 0:
            outgoing, row_weight = products(
                "degree", (0, 3), False, *to, "backward_start", 16, args, [((rows_dev // 2, LANES), F32)]
            )
        else:
            args = (*args, row_weight, row_parts)
            if last:
                args = (*args, *from_hbm(row_factor))
            (outgoing,) = products("plain", (0, 3), last, *to, "backward", message_rows, args)
        received = exchange(outgoing, "group")
        message = ((n_group, WIDTH // 2, LANES), F32) if last else ((n_group, col_half, LANES), BF16)
        copies, session, gram = call(
            functools.partial(sum_kernel, "last" if last else "plain", n_group, col_half, n_group),
            "session",
            [VMEM, VMEM],
            [message, panel_cols, ((message_rows, LANES), F32)],
            in_hbm=(0, 2),
        )(received, col_scale)
        gathered = exchange(copies, "group")
        if iteration == 0:
            col_factor, col_parts = factor_of(swap_cores(gram))
        elif not last:
            col_factor, col_parts = factor_of(swap_cores(gram), row_factor)
    col_factor, session, attendee = call(
        factor_last_kernel,
        "factor_last",
        [VMEM] * 4,
        [((LANES, LANES), F32), panel_cols, ((2 * row_half, WIDTH), F32)],
    )(*from_hbm(swap_cores(gram)), session, attendee, row_factor)
    (copies,) = call(
        functools.partial(gram_last_kernel, n_group, n_loop),
        "gram_last",
        [VMEM, VMEM],
        [((n_loop, 48, LANES), BF16)],
    )(gathered, col_factor)
    (session,) = call(
        functools.partial(last_kernel, n_loop),
        "session_out",
        [VMEM, VMEM],
        [((WIDTH, 2 * col_half), F32)],
    )(exchange(copies, "loop"), session)
    return (session.T[None], attendee[None])


def solution(mesh):
    in_specs = (
        P("group", "loop", None, None, None),
        P("group", "loop", None),
        P("group", "loop", None),
        P("group", "loop"),
        P("loop", "group", None),
    )
    out_specs = (P("loop", "group", None), P("group", "loop", None))
    return jax.shard_map(
        per_device, mesh=mesh, in_specs=in_specs, out_specs=out_specs, check_vma=False
    )
```

```python
import functools

import jax
import jax.numpy as jnp
from jax import lax
from jax.experimental import pallas as pl
from jax.experimental.pallas import tpu as pltpu
from jax.sharding import PartitionSpec as P

ITERS = 3
SIDE = 128
WIDTH = 64
LANES = 128
GRAM_ROWS = 48
DEGREE_ROWS = 16
F32 = jnp.float32
BF16 = jnp.bfloat16
HIGHEST = lax.Precision.HIGHEST

LOOP_ORDER = [k % 8 * 4 + k // 8 for k in range(32)]
LOOP_PLACE = [LOOP_ORDER.index(at) for at in range(32)]


def iota(shape, dim):
    return lax.broadcasted_iota(jnp.int32, shape, dim)


def halves_to_rows(packed):
    return jnp.concatenate([packed[:, :WIDTH], packed[:, WIDTH:]], axis=0)


def rows_to_halves(rows):
    half = rows.shape[0] // 2
    return jnp.concatenate([rows[:half], rows[half:]], axis=1)


def lanes_to_packed(row, half):
    shape = (half, LANES)
    spread = jnp.broadcast_to(row, shape)
    delta = iota(shape, 1) - iota(shape, 0)
    first = jnp.sum(jnp.where(delta == 0, spread, 0.0), axis=1, keepdims=True)
    last = jnp.sum(jnp.where(delta == half, spread, 0.0), axis=1, keepdims=True)
    return jnp.where(iota(shape, 1) < WIDTH, first, last)


def split_two(value):
    high = value.astype(BF16).astype(F32)
    return high, value - high


def diagonal_blocks(square):
    return square[:WIDTH, :WIDTH] + square[WIDTH:, WIDTH:]


def inverse_factor(gram):
    shape = (WIDTH, WIDTH)
    on_diagonal = iota(shape, 0) == iota(shape, 1)
    diagonal = jnp.where(on_diagonal, gram, 0.0)
    down = lax.rsqrt(jnp.sum(diagonal, axis=1, keepdims=True))
    across = lax.rsqrt(jnp.sum(diagonal, axis=0, keepdims=True))
    whole = jnp.concatenate([gram * down * across, jnp.where(on_diagonal, 1.0, 0.0)], axis=1)
    n_blocks = WIDTH // 8
    blocks = [whole[8 * b : 8 * b + 8] for b in range(n_blocks)]
    below = iota((8, LANES), 0)
    for p in range(n_blocks):
        spread = {
            b: [
                jnp.broadcast_to(blocks[b][:, 8 * p + j : 8 * p + j + 1], (8, LANES))
                for j in range(8)
            ]
            for b in range(p, n_blocks)
        }
        for k in range(0, 8, 2):
            own = list(spread[p])
            p00, p01, p11 = own[k][k : k + 1], own[k + 1][k : k + 1], own[k + 1][k + 1 : k + 2]
            inverse = 1.0 / (p00 * p11 - p01 * p01)
            q00, q01, q11 = p11 * inverse, p01 * inverse, p00 * inverse
            row0, row1 = blocks[p][k : k + 1], blocks[p][k + 1 : k + 2]
            for b in range(p, n_blocks):
                if b == p and k == 6:
                    continue
                column0, column1 = spread[b][k], spread[b][k + 1]
                if b == p:
                    column0 = jnp.where(below > k + 1, column0, 0.0)
                    column1 = jnp.where(below > k + 1, column1, 0.0)
                times0 = q00 * column0 - q01 * column1
                times1 = q11 * column1 - q01 * column0
                for j in range(k + 2, 8):
                    spread[b][j] = spread[b][j] - (
                        times0 * own[j][k : k + 1] + times1 * own[j][k + 1 : k + 2]
                    )
                blocks[b] = blocks[b] - (times0 * row0 + times1 * row1)
    whole = jnp.concatenate(blocks, axis=0)
    left, right = whole[:, :WIDTH], whole[:, WIDTH:]
    pivots = jnp.sum(jnp.where(on_diagonal, left, 0.0), axis=1, keepdims=True)
    beside = iota(shape, 0) == iota(shape, 1) + 1
    coupling = jnp.sum(jnp.where(beside, left, 0.0), axis=1, keepdims=True)
    above = jnp.concatenate([pivots[WIDTH - 1 :], pivots[: WIDTH - 1]], axis=0)
    right_above = jnp.concatenate([right[WIDTH - 1 :], right[: WIDTH - 1]], axis=0)
    odd = iota((WIDTH, 1), 0) % 2 == 1
    ratio = jnp.where(odd, coupling / above, 0.0)
    return (right - ratio * right_above) * lax.rsqrt(pivots - ratio * coupling) * across


def both_halves(inverse):
    zero = jnp.zeros((WIDTH, WIDTH), F32)
    return jnp.concatenate(
        [
            jnp.concatenate([inverse, zero], axis=1),
            jnp.concatenate([zero, inverse], axis=1),
        ],
        axis=0,
    )


def times_transposed(left, right):
    return lax.dot_general(
        left, right, (((1,), (1,)), ((), ())), precision=HIGHEST, preferred_element_type=F32
    )


def factor_parts(both):
    high, low = split_two(both.T)
    return jnp.concatenate([high, high, low], axis=0).astype(BF16)


def apply_parts(panel, parts):
    high, low = split_two(panel)
    mixed = jnp.concatenate([high, low, high], axis=1).astype(BF16)
    return jnp.dot(mixed, parts, preferred_element_type=F32)


def inverse_from_parts(parts):
    return (parts[:WIDTH, :WIDTH].astype(F32) + parts[2 * LANES :][:WIDTH, :WIDTH].astype(F32)).T


def dot_parts(left, right):
    (left_high, left_low), (right_high, right_low) = split_two(left), split_two(right)
    return jnp.dot(
        jnp.concatenate([left_high, left_low, left_high], axis=1).astype(BF16),
        jnp.concatenate([right_high, right_high, right_low], axis=0).astype(BF16),
        preferred_element_type=F32,
    )


def apply_to_gram(gram, inverse, exact=True):
    if not exact:
        return dot_parts(dot_parts(inverse, gram), inverse.T)
    turned = jnp.dot(inverse, gram, precision=HIGHEST, preferred_element_type=F32)
    return times_transposed(turned, inverse)


def gram_to_message(gram, whole):
    shape = (WIDTH, WIDTH)
    on_diagonal = iota(shape, 0) == iota(shape, 1)
    high, low = split_two(gram)
    mixed = jnp.where(iota(shape, 0) >= iota(shape, 1), high, low.T)
    if not whole:
        mixed = jnp.where(on_diagonal, gram * (1.0 + 2.0**-7), mixed)
    message = rows_to_halves(mixed)
    if whole:
        diagonal = jnp.sum(jnp.where(on_diagonal, low, 0.0), axis=0, keepdims=True)
        diagonal = jnp.concatenate([diagonal, diagonal], axis=1)
        message = jnp.concatenate([message, jnp.broadcast_to(diagonal, (16, LANES))], axis=0)
    return message.astype(BF16)


def message_to_gram(message):
    shape = (WIDTH, WIDTH)
    half = message.shape[0] // 2
    square = halves_to_rows(jnp.concatenate([message[:16], message[half : half + 16]], axis=0))
    on_diagonal = iota(shape, 0) == iota(shape, 1)
    whole = square if half == 16 else square + message[16:17, :WIDTH]
    return jnp.where(on_diagonal, whole, square + square.T)


def sum_per_block(target, sums, n_blocks):
    shape = (n_blocks, sums.shape[0])
    chosen = jnp.where(iota(shape, 0) == target, 1.0, 0.0)
    return jnp.dot(chosen, sums, precision=HIGHEST, preferred_element_type=F32)


def degree_kernel(index, values, start, copies):
    slots, half = values.shape[0], start.shape[1] // 2
    sums = [jnp.sum(values[t].astype(F32), axis=0, keepdims=True) for t in range(slots)]
    sums = jnp.concatenate(sums, axis=0)
    degree = sum_per_block(index[3:4, :slots], sums, copies.shape[1] - half)
    message = jnp.concatenate([rows_to_halves(start[...].T), degree], axis=0)
    for d in range(copies.shape[0]):
        copies[d] = message


def layout_kernel(row_half, col_half, index, values, forward, backward, row_degree, row_sum):
    ones = jnp.ones((8, SIDE), BF16)
    half = SIDE // 2
    slabs = [slice(at, at + row_half) for at in range(0, SIDE, row_half)]
    for t in range(values.shape[0]):
        tile = values[t]
        row_sum[t : t + 1] = lax.dot_general(
            ones, tile, (((1,), (1,)), ((), ())), preferred_element_type=F32
        )[:1]
        for at in range(0, half, row_half):
            forward[t, at : at + row_half, :SIDE] = tile[2 * at : 2 * at + row_half]
            forward[t, at : at + row_half, SIDE:] = tile[2 * at + row_half : 2 * at + 2 * row_half]
        order = slabs[0::2] + slabs[1::2]
        turned = jnp.concatenate([tile[rows] for rows in order], axis=0).T
        for at in range(0, half, col_half):
            backward[t, at : at + col_half, :SIDE] = turned[2 * at : 2 * at + col_half]
            backward[t, at : at + col_half, SIDE:] = turned[2 * at + col_half : 2 * at + 2 * col_half]
    slots = values.shape[0]
    row_degree[...] = sum_per_block(index[2:3, :slots], row_sum[...], row_degree.shape[0])


def product_kernel(kind, source, target, rows_from, n_to, rows_to, whole, from_pair, *refs):
    index, gathered, tiles, *refs, spread, total = refs
    if kind == "start":
        row_degree, out, weight, own_scale = refs
    elif kind == "degree":
        out, weight = refs
    else:
        weight, factor, out = refs
    half = SIDE // 2
    lane_low = iota((half, LANES), 1) < WIDTH
    n_blocks = total.shape[0] - 1
    per_block = half // rows_from

    if kind == "start":
        degree = 1.0 + jnp.sum(gathered[:, rows_from:, :], axis=0)

    grams = jnp.zeros((2 * LANES, LANES), F32)
    for b in range(n_blocks):
        rows = slice(b * half, (b + 1) * half)
        if kind == "start":
            packed_degree = lanes_to_packed(degree[b : b + 1], half)
            weight[rows] = packed_degree
            place = b % 2 * (n_blocks // 2) + b // 2
            panel = gathered[place, :rows_from] * lax.rsqrt(packed_degree)
            panel = panel.astype(BF16).astype(F32)
        else:
            places = [b * per_block + j for j in range(per_block)]
            if per_block > 1:
                places = [LOOP_PLACE[place] for place in places]
            parts = [gathered[place, :rows_from].astype(F32) for place in places]
            panel = parts[0] if per_block == 1 else jnp.concatenate(parts, axis=0)
        if kind == "degree":
            packs = []
            for place in places:
                pieces = gathered[place, rows_from:].astype(F32)
                packs.append(lanes_to_packed(jnp.sum(pieces[:3], axis=0, keepdims=True), rows_from))
            packed_degree = packs[0] if per_block == 1 else jnp.concatenate(packs, axis=0)
            weight[rows] = packed_degree
        turned = pltpu.roll(panel, WIDTH, 1)
        spread[b, :half] = jnp.where(lane_low, panel, 0.0).astype(BF16)
        spread[b, half : 2 * half] = jnp.where(lane_low, turned, 0.0).astype(BF16)
        spread[b, 2 * half : 3 * half] = jnp.where(lane_low, 0.0, turned).astype(BF16)
        spread[b, 3 * half :] = jnp.where(lane_low, 0.0, panel).astype(BF16)
        if kind != "start":
            high, low = split_two(panel * weight[rows])
            both = jnp.concatenate([high, low], axis=1).astype(BF16)
            grams = grams + lax.dot_general(
                both, panel.astype(BF16), (((0,), (0,)), ((), ())), preferred_element_type=F32
            )
        total[b] = jnp.zeros((half, LANES), F32)
    total[n_blocks] = jnp.zeros((half, LANES), F32)

    for t in range(tiles.shape[0]):
        total[index[target, t]] += jnp.dot(
            tiles[t], spread[index[source, t]], preferred_element_type=F32
        )

    if kind == "start":
        degrees = row_degree[...]
        parts = []
        for value in (degrees, pltpu.roll(degrees, WIDTH, 1)):
            high, rest = split_two(value)
            parts.append((high, *split_two(rest)))
        at = iota((DEGREE_ROWS, LANES), 0)
    else:
        gram = diagonal_blocks(grams[:LANES]) + diagonal_blocks(grams[LANES:])
        if kind == "plain":
            gram = apply_to_gram(gram, inverse_from_parts(factor[...]), exact=whole)
        message = gram_to_message(gram, whole)
        halves = [message[:16], message[16:32]]
        if whole:
            halves = [jnp.concatenate([part, message[32:]], axis=0) for part in halves]
        if from_pair:
            halves = [jnp.where(index[4, 1] == 0, *halves)] * 2
    if kind == "start":
        own = index[4, 0]
        own_scale[...] = lax.rsqrt(weight[pl.ds(own * rows_from, rows_from)])
    to_block = half // rows_to
    for b in range(n_blocks):
        product = total[b]
        if kind == "plain":
            product = apply_parts(product, factor[...])
        product = product.astype(BF16)
        for j in range(to_block):
            d = LOOP_PLACE[b * to_block + j] if to_block > 1 else b
            out[d, :rows_to] = product[j * rows_to : (j + 1) * rows_to]
            if kind == "start":
                high, middle, low = (part[b : b + 1] for part in parts[j])
                tail = jnp.where(at == 0, high, jnp.where(at == 1, middle, low))
                out[d, rows_to:] = jnp.where(at < 3, tail, 0.0).astype(BF16)
            else:
                out[d, rows_to:] = halves[b % 2]


def sum_kernel(kind, n_from, rows, n_copies, *refs):
    if kind == "degree":
        received, copies, panel_out, scale_out = refs
    else:
        received, scale_ref, copies, panel_out, gram_out = refs
    summed = received[0].astype(F32)
    for s in range(1, n_from):
        summed = summed + received[s].astype(F32)
    panel = summed[:rows]
    if kind == "degree":
        degree = 1.0 + jnp.sum(summed[rows : rows + 3], axis=0, keepdims=True)
        scale = lax.rsqrt(lanes_to_packed(degree, rows))
        scale_out[...] = scale
    else:
        scale = scale_ref[...]
        gram_out[...] = summed[rows:]
    panel = panel * scale
    panel_out[...] = panel
    if kind == "last":
        square = lax.dot_general(
            panel, panel, (((0,), (0,)), ((), ())), precision=HIGHEST, preferred_element_type=F32
        )
        message = rows_to_halves(diagonal_blocks(square))
    else:
        message = (panel * scale).astype(BF16)
    for d in range(n_copies):
        copies[d, : message.shape[0]] = message
    if kind == "degree":
        high, rest = split_two(degree)
        middle, low = split_two(rest)
        at = iota((DEGREE_ROWS, LANES), 0)
        tail = jnp.where(at == 0, high, jnp.where(at == 1, middle, jnp.where(at == 2, low, 0.0)))
        tail = tail.astype(BF16)
        for d in range(n_copies):
            copies[d, rows:] = tail


def factor_kernel(gram, parts):
    parts[...] = factor_parts(both_halves(inverse_factor(message_to_gram(gram[...]))))


def factor_last_kernel(gram, session, attendee, attendee_parts, factor, session_out, attendee_out):
    inverse = inverse_factor(message_to_gram(gram[...]))
    factor[...] = inverse
    both = both_halves(inverse)
    session_out[...] = times_transposed(session[...], both)
    turned = apply_parts(attendee[...], attendee_parts[...])
    attendee_out[...] = halves_to_rows(times_transposed(turned, both))


def gram_last_kernel(n_from, n_copies, received, factor, copies):
    summed = received[0]
    for s in range(1, n_from):
        summed = summed + received[s]
    gram = apply_to_gram(halves_to_rows(summed), factor[...])
    message = gram_to_message(gram, True)
    for d in range(n_copies):
        copies[d] = message


def last_kernel(n_from, received, panel, out):
    summed = received[0].astype(F32)
    for s in range(1, n_from):
        summed = summed + received[s].astype(F32)
    message = jnp.concatenate([summed[:16], summed[32:], summed[16:]], axis=0)
    both = both_halves(inverse_factor(message_to_gram(message)))
    out[...] = halves_to_rows(times_transposed(panel[...], both)).T


VMEM = pl.BlockSpec(memory_space=pltpu.VMEM)
SMEM = pl.BlockSpec(memory_space=pltpu.SMEM)


def call(kernel, name, in_specs, out_shapes, scratch=(), flops=10**8, in_hbm=()):
    return pl.pallas_call(
        kernel,
        name=name,
        in_specs=in_specs,
        out_specs=[VMEM] * len(out_shapes),
        out_shape=[
            pltpu.HBM(s, d) if i in in_hbm else jax.ShapeDtypeStruct(s, d)
            for i, (s, d) in enumerate(out_shapes)
        ],
        scratch_shapes=list(scratch),
        cost_estimate=pl.CostEstimate(flops=flops, bytes_accessed=2**20, transcendentals=0),
        compiler_params=pltpu.CompilerParams(vmem_limit_bytes=32 * 1024 * 1024),
    )


def from_hbm(*arrays):
    return [pltpu.with_memory_space_constraint(array, pltpu.HBM) for array in arrays]


def exchange(array, axis, groups=None):
    n, rows, lanes = array.shape
    return lax.all_to_all(
        array.reshape(n * rows, lanes),
        axis,
        split_axis=0,
        concat_axis=0,
        axis_index_groups=groups or ([LOOP_ORDER] if axis == "loop" else None),
        tiled=True,
    ).reshape(n, rows, lanes)


def per_device(tile_vals, tile_rows, tile_cols, tile_count, start_panel):
    values = tile_vals[0, 0]
    slots = values.shape[0]
    n_group, n_loop = lax.axis_size("group"), lax.axis_size("loop")
    rows_dev, cols_dev = 2048, 2048
    row_blocks, col_blocks = rows_dev // SIDE, cols_dev // SIDE
    row_half, col_half = rows_dev // n_loop // 2, cols_dev // n_group // 2
    half = SIDE // 2
    count, row_at, col_at = tile_count[0], tile_rows[0, 0], tile_cols[0, 0]

    alive = jnp.arange(slots) < count
    group = lax.axis_index("group")
    index = [row_at, col_at, jnp.where(alive, row_at, row_blocks)]
    index += [jnp.where(alive, col_at, col_blocks), jnp.pad(jnp.stack([group, group % 2]), (0, slots - 2))]
    index = jnp.pad(jnp.stack(index).astype(jnp.int32), ((0, 3), (0, LANES - slots)))
    (first,) = call(
        degree_kernel,
        "start_message",
        [VMEM] * 3,
        [((n_group // 2, col_half + col_blocks, LANES), F32)],
        in_hbm=(0,),
    )(index, *from_hbm(values, start_panel[0].T))
    pairs = [[i, i + 1] for i in range(0, n_group, 2)]
    gathered = exchange(first, "group", [list(range(core, n_group, 2)) for core in range(2)])
    gathered = lax.all_gather(gathered, "group", axis_index_groups=pairs, axis=0, tiled=True)
    forward, backward, row_degree = call(
        functools.partial(layout_kernel, row_half, col_half),
        "layouts",
        [VMEM] * 2,
        [
            ((slots, half, 2 * SIDE), BF16),
            ((slots, half, 2 * SIDE), BF16),
            ((row_blocks, SIDE), F32),
        ],
        [pltpu.VMEM((slots, SIDE), F32)],
    )(index, values)

    scratch = [
        pltpu.VMEM((col_blocks, 2 * SIDE, LANES), BF16),
        pltpu.VMEM((row_blocks + 1, half, LANES), F32),
    ]

    def factor_of(gram):
        return call(factor_kernel, "factor", [VMEM], [((3 * LANES, LANES), BF16)])(gram)[0]

    def products(kind, way, whole, rows_from, n_to, rows_to, name, extra_rows, args, others=()):
        return call(
            functools.partial(
                product_kernel, kind, *way, rows_from, n_to, rows_to, whole, n_to == n_loop
            ),
            name,
            [SMEM] + [VMEM] * len(args),
            [((n_to, rows_to + extra_rows, LANES), BF16), *others],
            scratch,
        )(index, *args)

    def swap_cores(half_message):
        return lax.all_gather(
            half_message, "group", axis_index_groups=pairs, axis=0, tiled=True
        )

    panel_rows = ((row_half, LANES), F32)
    panel_cols = ((col_half, LANES), F32)
    for iteration in range(ITERS):
        last = iteration == ITERS - 1
        args = (gathered, forward)
        to = (col_half, n_loop, row_half)
        if iteration == 0:
            outgoing, col_weight, col_scale = products(
                "start",
                (1, 2),
                False,
                *to,
                "forward_start",
                DEGREE_ROWS,
                (*args, row_degree),
                [((cols_dev // 2, LANES), F32), panel_cols],
            )
            received = exchange(outgoing, "loop")
            copies, attendee, row_scale = call(
                functools.partial(sum_kernel, "degree", n_loop, row_half, n_loop),
                "attendee_start",
                [VMEM],
                [((n_loop, row_half + DEGREE_ROWS, LANES), BF16), panel_rows, panel_rows],
            )(received)
        else:
            (outgoing,) = products(
                "plain", (1, 2), False, *to, "forward", 16, (*args, col_weight, col_parts)
            )
            received = exchange(outgoing, "loop")
            copies, attendee, gram = call(
                functools.partial(sum_kernel, "plain", n_loop, row_half, n_loop),
                "attendee",
                [VMEM, VMEM],
                [((n_loop, row_half, LANES), BF16), panel_rows, ((16, LANES), F32)],
                in_hbm=(0, 2),
            )(received, row_scale)
            row_parts = factor_of(swap_cores(gram))
        gathered = exchange(copies, "loop")
        args = (gathered, backward)
        to = (row_half, n_group, col_half)
        message_rows = 32 if last else 16
        if iteration == 0:
            outgoing, row_weight = products(
                "degree", (0, 3), False, *to, "backward_start", 16, args, [((rows_dev // 2, LANES), F32)]
            )
        else:
            args = (*args, row_weight, row_parts)
            (outgoing,) = products("plain", (0, 3), last, *to, "backward", message_rows, args)
        received = exchange(outgoing, "group")
        message = ((n_group, WIDTH // 2, LANES), F32) if last else ((n_group, col_half, LANES), BF16)
        copies, session, gram = call(
            functools.partial(sum_kernel, "last" if last else "plain", n_group, col_half, n_group),
            "session",
            [VMEM, VMEM],
            [message, panel_cols, ((message_rows, LANES), F32)],
            in_hbm=(0, 2),
        )(received, col_scale)
        gathered = exchange(copies, "group")
        if not last:
            col_parts = factor_of(swap_cores(gram))
    col_factor, session, attendee = call(
        factor_last_kernel,
        "factor_last",
        [VMEM] * 4,
        [((WIDTH, WIDTH), F32), panel_cols, ((2 * row_half, WIDTH), F32)],
    )(swap_cores(gram), session, attendee, row_parts)
    (copies,) = call(
        functools.partial(gram_last_kernel, n_group, n_loop),
        "gram_last",
        [VMEM, VMEM],
        [((n_loop, 48, LANES), BF16)],
    )(gathered, col_factor)
    (session,) = call(
        functools.partial(last_kernel, n_loop),
        "session_out",
        [VMEM, VMEM],
        [((WIDTH, 2 * col_half), F32)],
    )(exchange(copies, "loop"), session)
    return (session.T[None], attendee[None])


def solution(mesh):
    in_specs = (
        P("group", "loop", None, None, None),
        P("group", "loop", None),
        P("group", "loop", None),
        P("group", "loop"),
        P("loop", "group", None),
    )
    out_specs = (P("loop", "group", None), P("group", "loop", None))
    return jax.shard_map(
        per_device, mesh=mesh, in_specs=in_specs, out_specs=out_specs, check_vma=False
    )
```

```python
import functools

import jax
import jax.numpy as jnp
from jax import lax
from jax.experimental import pallas as pl
from jax.experimental.pallas import tpu as pltpu
from jax.sharding import PartitionSpec as P

ITERS = 3
SIDE = 128
WIDTH = 64
LANES = 128
DEGREE_ROWS = 16
F32 = jnp.float32
BF16 = jnp.bfloat16
HIGHEST = lax.Precision.HIGHEST

LOOP_ORDER = [k % 8 * 4 + k // 8 for k in range(32)]
LOOP_PLACE = [LOOP_ORDER.index(at) for at in range(32)]


def iota(shape, dim):
    return lax.broadcasted_iota(jnp.int32, shape, dim)


def halves_to_rows(packed):
    return jnp.concatenate([packed[:, :WIDTH], packed[:, WIDTH:]], axis=0)


def rows_to_halves(rows):
    half = rows.shape[0] // 2
    return jnp.concatenate([rows[:half], rows[half:]], axis=1)


def lanes_to_packed(row, half):
    shape = (half, LANES)
    spread = jnp.broadcast_to(row, shape)
    delta = iota(shape, 1) - iota(shape, 0)
    first = jnp.sum(jnp.where(delta == 0, spread, 0.0), axis=1, keepdims=True)
    last = jnp.sum(jnp.where(delta == half, spread, 0.0), axis=1, keepdims=True)
    return jnp.where(iota(shape, 1) < WIDTH, first, last)


def split_two(value):
    high = value.astype(BF16).astype(F32)
    return high, value - high


def diagonal_blocks(square):
    return square[:WIDTH, :WIDTH] + square[WIDTH:, WIDTH:]


def inverse_factor(gram):
    shape = (WIDTH, WIDTH)
    on_diagonal = iota(shape, 0) == iota(shape, 1)
    diagonal = jnp.where(on_diagonal, gram, 0.0)
    down = lax.rsqrt(jnp.sum(diagonal, axis=1, keepdims=True))
    across = lax.rsqrt(jnp.sum(diagonal, axis=0, keepdims=True))
    whole = jnp.concatenate([gram * down * across, jnp.where(on_diagonal, 1.0, 0.0)], axis=1)
    n_blocks = WIDTH // 8
    blocks = [whole[8 * b : 8 * b + 8] for b in range(n_blocks)]
    below = iota((8, LANES), 0)
    for p in range(n_blocks):
        spread = {
            b: [
                jnp.broadcast_to(blocks[b][:, 8 * p + j : 8 * p + j + 1], (8, LANES))
                for j in range(8)
            ]
            for b in range(p, n_blocks)
        }
        for k in range(0, 8, 2):
            own = list(spread[p])
            p00, p01, p11 = own[k][k : k + 1], own[k + 1][k : k + 1], own[k + 1][k + 1 : k + 2]
            inverse = 1.0 / (p00 * p11 - p01 * p01)
            q00, q01, q11 = p11 * inverse, p01 * inverse, p00 * inverse
            row0, row1 = blocks[p][k : k + 1], blocks[p][k + 1 : k + 2]
            for b in range(p, n_blocks):
                if b == p and k == 6:
                    continue
                column0, column1 = spread[b][k], spread[b][k + 1]
                if b == p:
                    column0 = jnp.where(below > k + 1, column0, 0.0)
                    column1 = jnp.where(below > k + 1, column1, 0.0)
                times0 = q00 * column0 - q01 * column1
                times1 = q11 * column1 - q01 * column0
                for j in range(k + 2, 8):
                    spread[b][j] = spread[b][j] - (
                        times0 * own[j][k : k + 1] + times1 * own[j][k + 1 : k + 2]
                    )
                blocks[b] = blocks[b] - (times0 * row0 + times1 * row1)
    whole = jnp.concatenate(blocks, axis=0)
    left, right = whole[:, :WIDTH], whole[:, WIDTH:]
    pivots = jnp.sum(jnp.where(on_diagonal, left, 0.0), axis=1, keepdims=True)
    beside = iota(shape, 0) == iota(shape, 1) + 1
    coupling = jnp.sum(jnp.where(beside, left, 0.0), axis=1, keepdims=True)
    above = jnp.concatenate([pivots[WIDTH - 1 :], pivots[: WIDTH - 1]], axis=0)
    right_above = jnp.concatenate([right[WIDTH - 1 :], right[: WIDTH - 1]], axis=0)
    odd = iota((WIDTH, 1), 0) % 2 == 1
    ratio = jnp.where(odd, coupling / above, 0.0)
    return (right - ratio * right_above) * lax.rsqrt(pivots - ratio * coupling) * across


def both_halves(inverse):
    zero = jnp.zeros((WIDTH, WIDTH), F32)
    return jnp.concatenate(
        [
            jnp.concatenate([inverse, zero], axis=1),
            jnp.concatenate([zero, inverse], axis=1),
        ],
        axis=0,
    )


def times_transposed(left, right):
    return lax.dot_general(
        left, right, (((1,), (1,)), ((), ())), precision=HIGHEST, preferred_element_type=F32
    )


def factor_parts(both):
    high, low = split_two(both.T)
    return jnp.concatenate([high, high, low], axis=0).astype(BF16)


def apply_parts(panel, parts):
    high, low = split_two(panel)
    mixed = jnp.concatenate([high, low, high], axis=1).astype(BF16)
    return jnp.dot(mixed, parts, preferred_element_type=F32)


def inverse_from_parts(parts):
    return (parts[:WIDTH, :WIDTH].astype(F32) + parts[2 * LANES :][:WIDTH, :WIDTH].astype(F32)).T


def dot_parts(left, right):
    (left_high, left_low), (right_high, right_low) = split_two(left), split_two(right)
    return jnp.dot(
        jnp.concatenate([left_high, left_low, left_high], axis=1).astype(BF16),
        jnp.concatenate([right_high, right_high, right_low], axis=0).astype(BF16),
        preferred_element_type=F32,
    )


def apply_to_gram(gram, inverse, exact=True):
    if not exact:
        return dot_parts(dot_parts(inverse, gram), inverse.T)
    turned = jnp.dot(inverse, gram, precision=HIGHEST, preferred_element_type=F32)
    return times_transposed(turned, inverse)


def gram_to_message(gram, whole):
    shape = (WIDTH, WIDTH)
    on_diagonal = iota(shape, 0) == iota(shape, 1)
    high, low = split_two(gram)
    mixed = jnp.where(iota(shape, 0) >= iota(shape, 1), high, low.T)
    if not whole:
        mixed = jnp.where(on_diagonal, gram * (1.0 + 2.0**-7), mixed)
    return rows_to_halves(mixed).astype(BF16)


def message_to_gram(message):
    shape = (WIDTH, WIDTH)
    square = halves_to_rows(message)
    on_diagonal = iota(shape, 0) == iota(shape, 1)
    return jnp.where(on_diagonal, square, square + square.T)


def sum_per_block(target, sums, n_blocks):
    shape = (n_blocks, sums.shape[0])
    chosen = jnp.where(iota(shape, 0) == target, 1.0, 0.0)
    return jnp.dot(chosen, sums, precision=HIGHEST, preferred_element_type=F32)


def degree_kernel(index, values, start, copies):
    slots, half = values.shape[0], start.shape[1] // 2
    sums = [jnp.sum(values[t].astype(F32), axis=0, keepdims=True) for t in range(slots)]
    sums = jnp.concatenate(sums, axis=0)
    degree = sum_per_block(index[3:4, :slots], sums, copies.shape[1] - half)
    message = jnp.concatenate([rows_to_halves(start[...].T), degree], axis=0)
    for d in range(copies.shape[0]):
        copies[d] = message


def layout_kernel(row_half, col_half, index, values, forward, backward, row_degree, row_sum):
    ones = jnp.ones((8, SIDE), BF16)
    half = SIDE // 2
    slabs = [slice(at, at + row_half) for at in range(0, SIDE, row_half)]
    for t in range(values.shape[0]):
        tile = values[t]
        row_sum[t : t + 1] = lax.dot_general(
            ones, tile, (((1,), (1,)), ((), ())), preferred_element_type=F32
        )[:1]
        for at in range(0, half, row_half):
            forward[t, at : at + row_half, :SIDE] = tile[2 * at : 2 * at + row_half]
            forward[t, at : at + row_half, SIDE:] = tile[2 * at + row_half : 2 * at + 2 * row_half]
        order = slabs[0::2] + slabs[1::2]
        turned = jnp.concatenate([tile[rows] for rows in order], axis=0).T
        for at in range(0, half, col_half):
            backward[t, at : at + col_half, :SIDE] = turned[2 * at : 2 * at + col_half]
            backward[t, at : at + col_half, SIDE:] = turned[2 * at + col_half : 2 * at + 2 * col_half]
    slots = values.shape[0]
    row_degree[...] = sum_per_block(index[2:3, :slots], row_sum[...], row_degree.shape[0])


def product_kernel(kind, source, target, rows_from, n_to, rows_to, whole, from_pair, *refs):
    index, gathered, tiles, *refs, spread, total = refs
    if kind == "start":
        row_degree, out, weight, own_scale = refs
    elif kind == "degree":
        out, weight = refs
    else:
        weight, factor, out = refs
    half = SIDE // 2
    lane_low = iota((half, LANES), 1) < WIDTH
    n_blocks = total.shape[0] - 1
    per_block = half // rows_from

    if kind == "start":
        degree = 1.0 + jnp.sum(gathered[:, rows_from:, :], axis=0)

    grams = jnp.zeros((2 * LANES, LANES), F32)
    for b in range(n_blocks):
        rows = slice(b * half, (b + 1) * half)
        if kind == "start":
            packed_degree = lanes_to_packed(degree[b : b + 1], half)
            weight[rows] = packed_degree
            place = b % 2 * (n_blocks // 2) + b // 2
            panel = gathered[place, :rows_from] * lax.rsqrt(packed_degree)
            panel = panel.astype(BF16).astype(F32)
        else:
            places = [b * per_block + j for j in range(per_block)]
            if per_block > 1:
                places = [LOOP_PLACE[place] for place in places]
            parts = [gathered[place, :rows_from].astype(F32) for place in places]
            panel = parts[0] if per_block == 1 else jnp.concatenate(parts, axis=0)
        if kind == "degree":
            packs = []
            for place in places:
                pieces = gathered[place, rows_from:].astype(F32)
                packs.append(lanes_to_packed(jnp.sum(pieces[:3], axis=0, keepdims=True), rows_from))
            packed_degree = packs[0] if per_block == 1 else jnp.concatenate(packs, axis=0)
            weight[rows] = packed_degree
        turned = pltpu.roll(panel, WIDTH, 1)
        spread[b, :half] = jnp.where(lane_low, panel, 0.0).astype(BF16)
        spread[b, half : 2 * half] = jnp.where(lane_low, turned, 0.0).astype(BF16)
        spread[b, 2 * half : 3 * half] = jnp.where(lane_low, 0.0, turned).astype(BF16)
        spread[b, 3 * half :] = jnp.where(lane_low, 0.0, panel).astype(BF16)
        if kind != "start":
            high, low = split_two(panel * weight[rows])
            both = jnp.concatenate([high, low], axis=1).astype(BF16)
            grams = grams + lax.dot_general(
                both, panel.astype(BF16), (((0,), (0,)), ((), ())), preferred_element_type=F32
            )
        total[b] = jnp.zeros((half, LANES), F32)
    total[n_blocks] = jnp.zeros((half, LANES), F32)

    for t in range(tiles.shape[0]):
        total[index[target, t]] += jnp.dot(
            tiles[t], spread[index[source, t]], preferred_element_type=F32
        )

    if kind == "start":
        degrees = row_degree[...]
        parts = []
        for value in (degrees, pltpu.roll(degrees, WIDTH, 1)):
            high, rest = split_two(value)
            parts.append((high, *split_two(rest)))
        at = iota((DEGREE_ROWS, LANES), 0)
    else:
        gram = diagonal_blocks(grams[:LANES]) + diagonal_blocks(grams[LANES:])
        if kind == "plain":
            gram = apply_to_gram(gram, inverse_from_parts(factor[...]), exact=whole)
        message = gram_to_message(gram, whole)
        halves = [message[:16], message[16:32]]
        if from_pair:
            halves = [jnp.where(index[4, 1] == 0, *halves)] * 2
    if kind == "start":
        own = index[4, 0]
        own_scale[...] = lax.rsqrt(weight[pl.ds(own * rows_from, rows_from)])
    to_block = half // rows_to
    for b in range(n_blocks):
        product = total[b]
        if kind == "plain":
            product = apply_parts(product, factor[...])
        product = product.astype(BF16)
        for j in range(to_block):
            d = LOOP_PLACE[b * to_block + j] if to_block > 1 else b
            out[d, :rows_to] = product[j * rows_to : (j + 1) * rows_to]
            if kind == "start":
                high, middle, low = (part[b : b + 1] for part in parts[j])
                tail = jnp.where(at == 0, high, jnp.where(at == 1, middle, low))
                out[d, rows_to:] = jnp.where(at < 3, tail, 0.0).astype(BF16)
            else:
                out[d, rows_to:] = halves[b % 2]


def sum_kernel(kind, n_from, rows, n_copies, *refs):
    if kind == "degree":
        received, copies, panel_out, scale_out = refs
    else:
        received, scale_ref, copies, panel_out, gram_out = refs
    summed = received[0].astype(F32)
    for s in range(1, n_from):
        summed = summed + received[s].astype(F32)
    panel = summed[:rows]
    if kind == "degree":
        degree = 1.0 + jnp.sum(summed[rows : rows + 3], axis=0, keepdims=True)
        scale = lax.rsqrt(lanes_to_packed(degree, rows))
        scale_out[...] = scale
    else:
        scale = scale_ref[...]
        gram_out[...] = summed[rows:]
    panel = panel * scale
    panel_out[...] = panel
    if kind == "last":
        square = lax.dot_general(
            panel, panel, (((0,), (0,)), ((), ())), precision=HIGHEST, preferred_element_type=F32
        )
        message = rows_to_halves(diagonal_blocks(square))
    else:
        message = (panel * scale).astype(BF16)
    for d in range(n_copies):
        copies[d, : message.shape[0]] = message
    if kind == "degree":
        high, rest = split_two(degree)
        middle, low = split_two(rest)
        at = iota((DEGREE_ROWS, LANES), 0)
        tail = jnp.where(at == 0, high, jnp.where(at == 1, middle, jnp.where(at == 2, low, 0.0)))
        tail = tail.astype(BF16)
        for d in range(n_copies):
            copies[d, rows:] = tail


def factor_kernel(gram, parts):
    parts[...] = factor_parts(both_halves(inverse_factor(message_to_gram(gram[...]))))


def factor_last_kernel(gram, session, attendee, attendee_parts, factor, session_out, attendee_out):
    inverse = inverse_factor(message_to_gram(gram[...]))
    factor[...] = inverse
    both = both_halves(inverse)
    session_out[...] = times_transposed(session[...], both)
    turned = apply_parts(attendee[...], attendee_parts[...])
    attendee_out[...] = halves_to_rows(times_transposed(turned, both))


def gram_last_kernel(n_from, n_copies, received, factor, copies):
    summed = received[0]
    for s in range(1, n_from):
        summed = summed + received[s]
    gram = apply_to_gram(halves_to_rows(summed), factor[...])
    message = gram_to_message(gram, True)
    for d in range(n_copies):
        copies[d] = message


def last_kernel(n_from, received, panel, out):
    summed = received[0].astype(F32)
    for s in range(1, n_from):
        summed = summed + received[s].astype(F32)
    both = both_halves(inverse_factor(message_to_gram(summed)))
    out[...] = halves_to_rows(times_transposed(panel[...], both)).T


VMEM = pl.BlockSpec(memory_space=pltpu.VMEM)
SMEM = pl.BlockSpec(memory_space=pltpu.SMEM)


def call(kernel, name, in_specs, out_shapes, scratch=(), flops=10**8, in_hbm=()):
    return pl.pallas_call(
        kernel,
        name=name,
        in_specs=in_specs,
        out_specs=[VMEM] * len(out_shapes),
        out_shape=[
            pltpu.HBM(s, d) if i in in_hbm else jax.ShapeDtypeStruct(s, d)
            for i, (s, d) in enumerate(out_shapes)
        ],
        scratch_shapes=list(scratch),
        cost_estimate=pl.CostEstimate(flops=flops, bytes_accessed=2**20, transcendentals=0),
        compiler_params=pltpu.CompilerParams(vmem_limit_bytes=32 * 1024 * 1024),
    )


def from_hbm(*arrays):
    return [pltpu.with_memory_space_constraint(array, pltpu.HBM) for array in arrays]


def exchange(array, axis, groups=None):
    n, rows, lanes = array.shape
    return lax.all_to_all(
        array.reshape(n * rows, lanes),
        axis,
        split_axis=0,
        concat_axis=0,
        axis_index_groups=groups or ([LOOP_ORDER] if axis == "loop" else None),
        tiled=True,
    ).reshape(n, rows, lanes)


def per_device(tile_vals, tile_rows, tile_cols, tile_count, start_panel):
    values = tile_vals[0, 0]
    slots = values.shape[0]
    n_group, n_loop = lax.axis_size("group"), lax.axis_size("loop")
    rows_dev, cols_dev = 2048, 2048
    row_blocks, col_blocks = rows_dev // SIDE, cols_dev // SIDE
    row_half, col_half = rows_dev // n_loop // 2, cols_dev // n_group // 2
    half = SIDE // 2
    count, row_at, col_at = tile_count[0], tile_rows[0, 0], tile_cols[0, 0]

    alive = jnp.arange(slots) < count
    group = lax.axis_index("group")
    index = [row_at, col_at, jnp.where(alive, row_at, row_blocks)]
    index += [jnp.where(alive, col_at, col_blocks), jnp.pad(jnp.stack([group, group % 2]), (0, slots - 2))]
    index = jnp.pad(jnp.stack(index).astype(jnp.int32), ((0, 3), (0, LANES - slots)))
    (first,) = call(
        degree_kernel,
        "start_message",
        [VMEM] * 3,
        [((n_group // 2, col_half + col_blocks, LANES), F32)],
        in_hbm=(0,),
    )(index, *from_hbm(values, start_panel[0].T))
    pairs = [[i, i + 1] for i in range(0, n_group, 2)]
    gathered = exchange(first, "group", [list(range(core, n_group, 2)) for core in range(2)])
    gathered = lax.all_gather(gathered, "group", axis_index_groups=pairs, axis=0, tiled=True)
    forward, backward, row_degree = call(
        functools.partial(layout_kernel, row_half, col_half),
        "layouts",
        [VMEM] * 2,
        [
            ((slots, half, 2 * SIDE), BF16),
            ((slots, half, 2 * SIDE), BF16),
            ((row_blocks, SIDE), F32),
        ],
        [pltpu.VMEM((slots, SIDE), F32)],
    )(index, values)

    scratch = [
        pltpu.VMEM((col_blocks, 2 * SIDE, LANES), BF16),
        pltpu.VMEM((row_blocks + 1, half, LANES), F32),
    ]

    def factor_of(gram):
        return call(factor_kernel, "factor", [VMEM], [((3 * LANES, LANES), BF16)])(gram)[0]

    def products(kind, way, whole, rows_from, n_to, rows_to, name, extra_rows, args, others=()):
        return call(
            functools.partial(
                product_kernel, kind, *way, rows_from, n_to, rows_to, whole, n_to == n_loop
            ),
            name,
            [SMEM] + [VMEM] * len(args),
            [((n_to, rows_to + extra_rows, LANES), BF16), *others],
            scratch,
        )(index, *args)

    def swap_cores(half_message):
        return lax.all_gather(
            half_message, "group", axis_index_groups=pairs, axis=0, tiled=True
        )

    panel_rows = ((row_half, LANES), F32)
    panel_cols = ((col_half, LANES), F32)
    for iteration in range(ITERS):
        last = iteration == ITERS - 1
        args = (gathered, forward)
        to = (col_half, n_loop, row_half)
        if iteration == 0:
            outgoing, col_weight, col_scale = products(
                "start",
                (1, 2),
                False,
                *to,
                "forward_start",
                DEGREE_ROWS,
                (*args, row_degree),
                [((cols_dev // 2, LANES), F32), panel_cols],
            )
            received = exchange(outgoing, "loop")
            copies, attendee, row_scale = call(
                functools.partial(sum_kernel, "degree", n_loop, row_half, n_loop),
                "attendee_start",
                [VMEM],
                [((n_loop, row_half + DEGREE_ROWS, LANES), BF16), panel_rows, panel_rows],
            )(received)
        else:
            (outgoing,) = products(
                "plain", (1, 2), False, *to, "forward", 16, (*args, col_weight, col_parts)
            )
            received = exchange(outgoing, "loop")
            copies, attendee, gram = call(
                functools.partial(sum_kernel, "plain", n_loop, row_half, n_loop),
                "attendee",
                [VMEM, VMEM],
                [((n_loop, row_half, LANES), BF16), panel_rows, ((16, LANES), F32)],
                in_hbm=(0, 2),
            )(received, row_scale)
            row_parts = factor_of(swap_cores(gram))
        gathered = exchange(copies, "loop")
        args = (gathered, backward)
        to = (row_half, n_group, col_half)
        if iteration == 0:
            outgoing, row_weight = products(
                "degree", (0, 3), False, *to, "backward_start", 16, args, [((rows_dev // 2, LANES), F32)]
            )
        else:
            args = (*args, row_weight, row_parts)
            (outgoing,) = products("plain", (0, 3), last, *to, "backward", 16, args)
        received = exchange(outgoing, "group")
        message = ((n_group, WIDTH // 2, LANES), F32) if last else ((n_group, col_half, LANES), BF16)
        copies, session, gram = call(
            functools.partial(sum_kernel, "last" if last else "plain", n_group, col_half, n_group),
            "session",
            [VMEM, VMEM],
            [message, panel_cols, ((16, LANES), F32)],
            in_hbm=(0, 2),
        )(received, col_scale)
        gathered = exchange(copies, "group")
        if not last:
            col_parts = factor_of(swap_cores(gram))
    col_factor, session, attendee = call(
        factor_last_kernel,
        "factor_last",
        [VMEM] * 4,
        [((WIDTH, WIDTH), F32), panel_cols, ((2 * row_half, WIDTH), F32)],
    )(swap_cores(gram), session, attendee, row_parts)
    (copies,) = call(
        functools.partial(gram_last_kernel, n_group, n_loop),
        "gram_last",
        [VMEM, VMEM],
        [((n_loop, 32, LANES), BF16)],
    )(gathered, col_factor)
    (session,) = call(
        functools.partial(last_kernel, n_loop),
        "session_out",
        [VMEM, VMEM],
        [((WIDTH, 2 * col_half), F32)],
    )(exchange(copies, "loop"), session)
    return (session.T[None], attendee[None])


def solution(mesh):
    in_specs = (
        P("group", "loop", None, None, None),
        P("group", "loop", None),
        P("group", "loop", None),
        P("group", "loop"),
        P("loop", "group", None),
    )
    out_specs = (P("loop", "group", None), P("group", "loop", None))
    return jax.shard_map(
        per_device, mesh=mesh, in_specs=in_specs, out_specs=out_specs, check_vma=False
    )
```

```python
import functools

import jax
import jax.numpy as jnp
from jax import lax
from jax.experimental import pallas as pl
from jax.experimental.pallas import tpu as pltpu
from jax.sharding import PartitionSpec as P

ITERS = 3
SIDE = 128
WIDTH = 64
LANES = 128
DEGREE_ROWS = 16
F32 = jnp.float32
BF16 = jnp.bfloat16
HIGHEST = lax.Precision.HIGHEST

LOOP_ORDER = [k % 8 * 4 + k // 8 for k in range(32)]
LOOP_PLACE = [LOOP_ORDER.index(at) for at in range(32)]


def iota(shape, dim):
    return lax.broadcasted_iota(jnp.int32, shape, dim)


def halves_to_rows(packed):
    return jnp.concatenate([packed[:, :WIDTH], packed[:, WIDTH:]], axis=0)


def rows_to_halves(rows):
    half = rows.shape[0] // 2
    return jnp.concatenate([rows[:half], rows[half:]], axis=1)


def lanes_to_packed(row, half):
    shape = (half, LANES)
    spread = jnp.broadcast_to(row, shape)
    delta = iota(shape, 1) - iota(shape, 0)
    first = jnp.sum(jnp.where(delta == 0, spread, 0.0), axis=1, keepdims=True)
    last = jnp.sum(jnp.where(delta == half, spread, 0.0), axis=1, keepdims=True)
    return jnp.where(iota(shape, 1) < WIDTH, first, last)


def split_two(value):
    high = value.astype(BF16).astype(F32)
    return high, value - high


def diagonal_blocks(square):
    return square[:WIDTH, :WIDTH] + square[WIDTH:, WIDTH:]


def inverse_factor(gram):
    shape = (WIDTH, WIDTH)
    on_diagonal = iota(shape, 0) == iota(shape, 1)
    diagonal = jnp.where(on_diagonal, gram, 0.0)
    down = lax.rsqrt(jnp.sum(diagonal, axis=1, keepdims=True))
    across = lax.rsqrt(jnp.sum(diagonal, axis=0, keepdims=True))
    whole = jnp.concatenate([gram * down * across, jnp.where(on_diagonal, 1.0, 0.0)], axis=1)
    n_blocks = WIDTH // 8
    blocks = [whole[8 * b : 8 * b + 8] for b in range(n_blocks)]
    below = iota((8, LANES), 0)
    for p in range(n_blocks):
        spread = {
            b: [
                jnp.broadcast_to(blocks[b][:, 8 * p + j : 8 * p + j + 1], (8, LANES))
                for j in range(8)
            ]
            for b in range(p, n_blocks)
        }
        for k in range(0, 8, 2):
            own = list(spread[p])
            p00, p01, p11 = own[k][k : k + 1], own[k + 1][k : k + 1], own[k + 1][k + 1 : k + 2]
            inverse = 1.0 / (p00 * p11 - p01 * p01)
            q00, q01, q11 = p11 * inverse, p01 * inverse, p00 * inverse
            row0, row1 = blocks[p][k : k + 1], blocks[p][k + 1 : k + 2]
            for b in range(p, n_blocks):
                if b == p and k == 6:
                    continue
                column0, column1 = spread[b][k], spread[b][k + 1]
                if b == p:
                    column0 = jnp.where(below > k + 1, column0, 0.0)
                    column1 = jnp.where(below > k + 1, column1, 0.0)
                times0 = q00 * column0 - q01 * column1
                times1 = q11 * column1 - q01 * column0
                for j in range(k + 2, 8):
                    spread[b][j] = spread[b][j] - (
                        times0 * own[j][k : k + 1] + times1 * own[j][k + 1 : k + 2]
                    )
                blocks[b] = blocks[b] - (times0 * row0 + times1 * row1)
    whole = jnp.concatenate(blocks, axis=0)
    left, right = whole[:, :WIDTH], whole[:, WIDTH:]
    pivots = jnp.sum(jnp.where(on_diagonal, left, 0.0), axis=1, keepdims=True)
    beside = iota(shape, 0) == iota(shape, 1) + 1
    coupling = jnp.sum(jnp.where(beside, left, 0.0), axis=1, keepdims=True)
    above = jnp.concatenate([pivots[WIDTH - 1 :], pivots[: WIDTH - 1]], axis=0)
    right_above = jnp.concatenate([right[WIDTH - 1 :], right[: WIDTH - 1]], axis=0)
    odd = iota((WIDTH, 1), 0) % 2 == 1
    ratio = jnp.where(odd, coupling / above, 0.0)
    return (right - ratio * right_above) * lax.rsqrt(pivots - ratio * coupling) * across


def both_halves(inverse):
    zero = jnp.zeros((WIDTH, WIDTH), F32)
    return jnp.concatenate(
        [
            jnp.concatenate([inverse, zero], axis=1),
            jnp.concatenate([zero, inverse], axis=1),
        ],
        axis=0,
    )


def times_transposed(left, right):
    return lax.dot_general(
        left, right, (((1,), (1,)), ((), ())), precision=HIGHEST, preferred_element_type=F32
    )


def factor_parts(both):
    high, low = split_two(both.T)
    return jnp.concatenate([high, high, low], axis=0).astype(BF16)


def apply_parts(panel, parts):
    high, low = split_two(panel)
    mixed = jnp.concatenate([high, low, high], axis=1).astype(BF16)
    return jnp.dot(mixed, parts, preferred_element_type=F32)


def inverse_from_parts(parts):
    return (parts[:WIDTH, :WIDTH].astype(F32) + parts[2 * LANES :][:WIDTH, :WIDTH].astype(F32)).T


def dot_parts(left, right):
    (left_high, left_low), (right_high, right_low) = split_two(left), split_two(right)
    return jnp.dot(
        jnp.concatenate([left_high, left_low, left_high], axis=1).astype(BF16),
        jnp.concatenate([right_high, right_high, right_low], axis=0).astype(BF16),
        preferred_element_type=F32,
    )


def apply_to_gram(gram, inverse, exact=True):
    if not exact:
        return dot_parts(dot_parts(inverse, gram), inverse.T)
    turned = jnp.dot(inverse, gram, precision=HIGHEST, preferred_element_type=F32)
    return times_transposed(turned, inverse)


def gram_to_message(gram, whole):
    shape = (WIDTH, WIDTH)
    on_diagonal = iota(shape, 0) == iota(shape, 1)
    high, low = split_two(gram)
    mixed = jnp.where(iota(shape, 0) >= iota(shape, 1), high, low.T)
    if not whole:
        mixed = jnp.where(on_diagonal, gram * (1.0 + 2.0**-7), mixed)
    return rows_to_halves(mixed).astype(BF16)


def message_to_gram(message):
    shape = (WIDTH, WIDTH)
    square = halves_to_rows(message)
    on_diagonal = iota(shape, 0) == iota(shape, 1)
    return jnp.where(on_diagonal, square, square + square.T)


def sum_per_block(target, sums, n_blocks):
    shape = (n_blocks, sums.shape[0])
    chosen = jnp.where(iota(shape, 0) == target, 1.0, 0.0)
    return jnp.dot(chosen, sums, precision=HIGHEST, preferred_element_type=F32)


def degree_kernel(index, values, start, copies):
    slots, half = values.shape[0], start.shape[1] // 2
    sums = [jnp.sum(values[t].astype(F32), axis=0, keepdims=True) for t in range(slots)]
    sums = jnp.concatenate(sums, axis=0)
    degree = sum_per_block(index[3:4, :slots], sums, copies.shape[1] - half)
    message = jnp.concatenate([rows_to_halves(start[...].T), degree], axis=0)
    for d in range(copies.shape[0]):
        copies[d] = message


def layout_kernel(row_half, col_half, index, values, forward, backward, row_degree, row_sum):
    ones = jnp.ones((8, SIDE), BF16)
    half = SIDE // 2
    slabs = [slice(at, at + row_half) for at in range(0, SIDE, row_half)]
    for t in range(values.shape[0]):
        tile = values[t]
        row_sum[t : t + 1] = lax.dot_general(
            ones, tile, (((1,), (1,)), ((), ())), preferred_element_type=F32
        )[:1]
        for at in range(0, half, row_half):
            forward[t, at : at + row_half, :SIDE] = tile[2 * at : 2 * at + row_half]
            forward[t, at : at + row_half, SIDE:] = tile[2 * at + row_half : 2 * at + 2 * row_half]
        order = slabs[0::2] + slabs[1::2]
        turned = jnp.concatenate([tile[rows] for rows in order], axis=0).T
        for at in range(0, half, col_half):
            backward[t, at : at + col_half, :SIDE] = turned[2 * at : 2 * at + col_half]
            backward[t, at : at + col_half, SIDE:] = turned[2 * at + col_half : 2 * at + 2 * col_half]
    slots = values.shape[0]
    row_degree[...] = sum_per_block(index[2:3, :slots], row_sum[...], row_degree.shape[0])


def product_kernel(kind, source, target, rows_from, n_to, rows_to, whole, from_pair, *refs):
    index, gathered, tiles, *refs, spread, total = refs
    if kind == "start":
        row_degree, out, weight, own_scale = refs
    elif kind == "degree":
        out, weight = refs
    else:
        weight, factor, out = refs
    half = SIDE // 2
    lane_low = iota((half, LANES), 1) < WIDTH
    n_blocks = total.shape[0] - 1
    per_block = half // rows_from

    if kind == "start":
        degree = 1.0 + jnp.sum(gathered[:, rows_from:, :], axis=0)

    grams = jnp.zeros((2 * LANES, LANES), F32)
    for b in range(n_blocks):
        rows = slice(b * half, (b + 1) * half)
        if kind == "start":
            packed_degree = lanes_to_packed(degree[b : b + 1], half)
            weight[rows] = packed_degree
            place = b % 2 * (n_blocks // 2) + b // 2
            panel = gathered[place, :rows_from] * lax.rsqrt(packed_degree)
            panel = panel.astype(BF16).astype(F32)
        else:
            places = [b * per_block + j for j in range(per_block)]
            if per_block > 1:
                places = [LOOP_PLACE[place] for place in places]
            parts = [gathered[place, :rows_from].astype(F32) for place in places]
            panel = parts[0] if per_block == 1 else jnp.concatenate(parts, axis=0)
        if kind == "degree":
            packs = []
            for place in places:
                pieces = gathered[place, rows_from:].astype(F32)
                packs.append(lanes_to_packed(jnp.sum(pieces[:3], axis=0, keepdims=True), rows_from))
            packed_degree = packs[0] if per_block == 1 else jnp.concatenate(packs, axis=0)
            weight[rows] = packed_degree
        turned = pltpu.roll(panel, WIDTH, 1)
        spread[b, :half] = jnp.where(lane_low, panel, 0.0).astype(BF16)
        spread[b, half : 2 * half] = jnp.where(lane_low, turned, 0.0).astype(BF16)
        spread[b, 2 * half : 3 * half] = jnp.where(lane_low, 0.0, turned).astype(BF16)
        spread[b, 3 * half :] = jnp.where(lane_low, 0.0, panel).astype(BF16)
        if kind != "start":
            high, low = split_two(panel * weight[rows])
            both = jnp.concatenate([high, low], axis=1).astype(BF16)
            grams = grams + lax.dot_general(
                both, panel.astype(BF16), (((0,), (0,)), ((), ())), preferred_element_type=F32
            )
        total[b] = jnp.zeros((half, LANES), F32)
    total[n_blocks] = jnp.zeros((half, LANES), F32)

    for t in range(tiles.shape[0]):
        total[index[target, t]] += jnp.dot(
            tiles[t], spread[index[source, t]], preferred_element_type=F32
        )

    if kind == "start":
        degrees = row_degree[...]
        parts = []
        for value in (degrees, pltpu.roll(degrees, WIDTH, 1)):
            high, rest = split_two(value)
            parts.append((high, *split_two(rest)))
        at = iota((DEGREE_ROWS, LANES), 0)
    else:
        gram = diagonal_blocks(grams[:LANES]) + diagonal_blocks(grams[LANES:])
        if kind == "plain":
            gram = apply_to_gram(gram, inverse_from_parts(factor[...]), exact=whole)
        message = gram_to_message(gram, whole)
        halves = [message[:16], message[16:32]]
        if from_pair:
            halves = [jnp.where(index[4, 1] == 0, *halves)] * 2
    if kind == "start":
        own = index[4, 0]
        own_scale[...] = lax.rsqrt(weight[pl.ds(own * rows_from, rows_from)])
    to_block = half // rows_to
    for b in range(n_blocks):
        product = total[b]
        if kind == "plain":
            product = apply_parts(product, factor[...])
        product = product.astype(BF16)
        for j in range(to_block):
            d = LOOP_PLACE[b * to_block + j] if to_block > 1 else b
            out[d, :rows_to] = product[j * rows_to : (j + 1) * rows_to]
            if kind == "start":
                high, middle, low = (part[b : b + 1] for part in parts[j])
                tail = jnp.where(at == 0, high, jnp.where(at == 1, middle, low))
                out[d, rows_to:] = jnp.where(at < 3, tail, 0.0).astype(BF16)
            else:
                out[d, rows_to:] = halves[b % 2]


def sum_kernel(kind, n_from, rows, n_copies, *refs):
    if kind == "degree":
        received, copies, panel_out, scale_out = refs
    else:
        received, scale_ref, copies, panel_out, gram_out = refs
    summed = received[0].astype(F32)
    for s in range(1, n_from):
        summed = summed + received[s].astype(F32)
    panel = summed[:rows]
    if kind == "degree":
        degree = 1.0 + jnp.sum(summed[rows : rows + 3], axis=0, keepdims=True)
        scale = lax.rsqrt(lanes_to_packed(degree, rows))
        scale_out[...] = scale
    else:
        scale = scale_ref[...]
        gram_out[...] = summed[rows:]
    panel = panel * scale
    panel_out[...] = panel
    if kind == "last":
        square = lax.dot_general(
            panel, panel, (((0,), (0,)), ((), ())), precision=HIGHEST, preferred_element_type=F32
        )
        message = gram_to_message(diagonal_blocks(square), True)
    else:
        message = (panel * scale).astype(BF16)
    for d in range(n_copies):
        copies[d, : message.shape[0]] = message
    if kind == "degree":
        high, rest = split_two(degree)
        middle, low = split_two(rest)
        at = iota((DEGREE_ROWS, LANES), 0)
        tail = jnp.where(at == 0, high, jnp.where(at == 1, middle, jnp.where(at == 2, low, 0.0)))
        tail = tail.astype(BF16)
        for d in range(n_copies):
            copies[d, rows:] = tail


def factor_kernel(gram, parts):
    parts[...] = factor_parts(both_halves(inverse_factor(message_to_gram(gram[...]))))


def factor_last_kernel(gram, session, attendee, attendee_parts, factor, session_out, attendee_out):
    inverse = inverse_factor(message_to_gram(gram[...]))
    factor[...] = inverse
    both = both_halves(inverse)
    session_out[...] = times_transposed(session[...], both)
    turned = apply_parts(attendee[...], attendee_parts[...])
    attendee_out[...] = halves_to_rows(times_transposed(turned, both))


def gram_last_kernel(n_from, n_copies, received, factor, copies):
    summed = received[0].astype(F32)
    for s in range(1, n_from):
        summed = summed + received[s].astype(F32)
    gram = apply_to_gram(message_to_gram(summed), factor[...])
    message = gram_to_message(gram, True)
    for d in range(n_copies):
        copies[d] = message


def last_kernel(n_from, received, panel, out):
    summed = received[0].astype(F32)
    for s in range(1, n_from):
        summed = summed + received[s].astype(F32)
    both = both_halves(inverse_factor(message_to_gram(summed)))
    out[...] = halves_to_rows(times_transposed(panel[...], both)).T


VMEM = pl.BlockSpec(memory_space=pltpu.VMEM)
SMEM = pl.BlockSpec(memory_space=pltpu.SMEM)


def call(kernel, name, in_specs, out_shapes, scratch=(), flops=10**8, in_hbm=()):
    return pl.pallas_call(
        kernel,
        name=name,
        in_specs=in_specs,
        out_specs=[VMEM] * len(out_shapes),
        out_shape=[
            pltpu.HBM(s, d) if i in in_hbm else jax.ShapeDtypeStruct(s, d)
            for i, (s, d) in enumerate(out_shapes)
        ],
        scratch_shapes=list(scratch),
        cost_estimate=pl.CostEstimate(flops=flops, bytes_accessed=2**20, transcendentals=0),
        compiler_params=pltpu.CompilerParams(vmem_limit_bytes=32 * 1024 * 1024),
    )


def from_hbm(*arrays):
    return [pltpu.with_memory_space_constraint(array, pltpu.HBM) for array in arrays]


def exchange(array, axis, groups=None):
    n, rows, lanes = array.shape
    return lax.all_to_all(
        array.reshape(n * rows, lanes),
        axis,
        split_axis=0,
        concat_axis=0,
        axis_index_groups=groups or ([LOOP_ORDER] if axis == "loop" else None),
        tiled=True,
    ).reshape(n, rows, lanes)


def per_device(tile_vals, tile_rows, tile_cols, tile_count, start_panel):
    values = tile_vals[0, 0]
    slots = values.shape[0]
    n_group, n_loop = lax.axis_size("group"), lax.axis_size("loop")
    rows_dev, cols_dev = 2048, 2048
    row_blocks, col_blocks = rows_dev // SIDE, cols_dev // SIDE
    row_half, col_half = rows_dev // n_loop // 2, cols_dev // n_group // 2
    half = SIDE // 2
    count, row_at, col_at = tile_count[0], tile_rows[0, 0], tile_cols[0, 0]

    alive = jnp.arange(slots) < count
    group = lax.axis_index("group")
    index = [row_at, col_at, jnp.where(alive, row_at, row_blocks)]
    index += [jnp.where(alive, col_at, col_blocks), jnp.pad(jnp.stack([group, group % 2]), (0, slots - 2))]
    index = jnp.pad(jnp.stack(index).astype(jnp.int32), ((0, 3), (0, LANES - slots)))
    (first,) = call(
        degree_kernel,
        "start_message",
        [VMEM] * 3,
        [((n_group // 2, col_half + col_blocks, LANES), F32)],
        in_hbm=(0,),
    )(index, *from_hbm(values, start_panel[0].T))
    pairs = [[i, i + 1] for i in range(0, n_group, 2)]
    gathered = exchange(first, "group", [list(range(core, n_group, 2)) for core in range(2)])
    gathered = lax.all_gather(gathered, "group", axis_index_groups=pairs, axis=0, tiled=True)
    forward, backward, row_degree = call(
        functools.partial(layout_kernel, row_half, col_half),
        "layouts",
        [VMEM] * 2,
        [
            ((slots, half, 2 * SIDE), BF16),
            ((slots, half, 2 * SIDE), BF16),
            ((row_blocks, SIDE), F32),
        ],
        [pltpu.VMEM((slots, SIDE), F32)],
    )(index, values)

    scratch = [
        pltpu.VMEM((col_blocks, 2 * SIDE, LANES), BF16),
        pltpu.VMEM((row_blocks + 1, half, LANES), F32),
    ]

    def factor_of(gram):
        return call(factor_kernel, "factor", [VMEM], [((3 * LANES, LANES), BF16)])(gram)[0]

    def products(kind, way, whole, rows_from, n_to, rows_to, name, extra_rows, args, others=()):
        return call(
            functools.partial(
                product_kernel, kind, *way, rows_from, n_to, rows_to, whole, n_to == n_loop
            ),
            name,
            [SMEM] + [VMEM] * len(args),
            [((n_to, rows_to + extra_rows, LANES), BF16), *others],
            scratch,
        )(index, *args)

    def swap_cores(half_message):
        return lax.all_gather(
            half_message, "group", axis_index_groups=pairs, axis=0, tiled=True
        )

    panel_rows = ((row_half, LANES), F32)
    panel_cols = ((col_half, LANES), F32)
    for iteration in range(ITERS):
        last = iteration == ITERS - 1
        args = (gathered, forward)
        to = (col_half, n_loop, row_half)
        if iteration == 0:
            outgoing, col_weight, col_scale = products(
                "start",
                (1, 2),
                False,
                *to,
                "forward_start",
                DEGREE_ROWS,
                (*args, row_degree),
                [((cols_dev // 2, LANES), F32), panel_cols],
            )
            received = exchange(outgoing, "loop")
            copies, attendee, row_scale = call(
                functools.partial(sum_kernel, "degree", n_loop, row_half, n_loop),
                "attendee_start",
                [VMEM],
                [((n_loop, row_half + DEGREE_ROWS, LANES), BF16), panel_rows, panel_rows],
            )(received)
        else:
            (outgoing,) = products(
                "plain", (1, 2), False, *to, "forward", 16, (*args, col_weight, col_parts)
            )
            received = exchange(outgoing, "loop")
            copies, attendee, gram = call(
                functools.partial(sum_kernel, "plain", n_loop, row_half, n_loop),
                "attendee",
                [VMEM, VMEM],
                [((n_loop, row_half, LANES), BF16), panel_rows, ((16, LANES), F32)],
                in_hbm=(0, 2),
            )(received, row_scale)
            row_parts = factor_of(swap_cores(gram))
        gathered = exchange(copies, "loop")
        args = (gathered, backward)
        to = (row_half, n_group, col_half)
        if iteration == 0:
            outgoing, row_weight = products(
                "degree", (0, 3), False, *to, "backward_start", 16, args, [((rows_dev // 2, LANES), F32)]
            )
        else:
            args = (*args, row_weight, row_parts)
            (outgoing,) = products("plain", (0, 3), last, *to, "backward", 16, args)
        received = exchange(outgoing, "group")
        message = ((n_group, WIDTH // 2, LANES), BF16) if last else ((n_group, col_half, LANES), BF16)
        copies, session, gram = call(
            functools.partial(sum_kernel, "last" if last else "plain", n_group, col_half, n_group),
            "session",
            [VMEM, VMEM],
            [message, panel_cols, ((16, LANES), F32)],
            in_hbm=(0, 2),
        )(received, col_scale)
        gathered = exchange(copies, "group")
        if not last:
            col_parts = factor_of(swap_cores(gram))
    col_factor, session, attendee = call(
        factor_last_kernel,
        "factor_last",
        [VMEM] * 4,
        [((WIDTH, WIDTH), F32), panel_cols, ((2 * row_half, WIDTH), F32)],
    )(swap_cores(gram), session, attendee, row_parts)
    (copies,) = call(
        functools.partial(gram_last_kernel, n_group, n_loop),
        "gram_last",
        [VMEM, VMEM],
        [((n_loop, 32, LANES), BF16)],
    )(gathered, col_factor)
    (session,) = call(
        functools.partial(last_kernel, n_loop),
        "session_out",
        [VMEM, VMEM],
        [((WIDTH, 2 * col_half), F32)],
    )(exchange(copies, "loop"), session)
    return (session.T[None], attendee[None])


def solution(mesh):
    in_specs = (
        P("group", "loop", None, None, None),
        P("group", "loop", None),
        P("group", "loop", None),
        P("group", "loop"),
        P("loop", "group", None),
    )
    out_specs = (P("loop", "group", None), P("group", "loop", None))
    return jax.shard_map(
        per_device, mesh=mesh, in_specs=in_specs, out_specs=out_specs, check_vma=False
    )
```
